256 devices in a mesh: level: 8 (over y, core), row: 32 (over z, x).
Axes of the slice: x: 4, y: 4, z: 8, core: 2. Of those that a mesh axis runs over, the one named last changes fastest.
Arguments:
- points: float32 [8, 512, 3, 512], P('level', 'row'), may hold values from 0.02 to 4.5, as said below
- panels: float32 [8, 512, 512, 128], P('level', 'row'), may hold values from -6 to 6
- near_nodes: int32 [8, 512, 2], P('level', 'row'), may hold values from 0 to 47
- skeleton: int32 [8, 512, 128], P('level', 'row'), may hold values from 0 to 511, as said below
- owner_map: int32 [8, 512, 1], P('level', 'row'), may hold values from 0 to 31; in each aligned block of 16 rows (0 to 15, 16 to 31, ..., all dimensions but the last counted through in order) at most 2 rows name the same one
- transfer: float32 [8, 512, 128, 128], P('level', 'row'), may hold values from -0.375 to 0.375
- coupling: float32 [8, 4096, 128], P('level', 'row'), as said below
Outputs:
- solved: float32 [8, 512, 128, 128], P('level', 'row')
The draws below stay inside these ranges and needn't reach their ends.
Inputs may be any that keep to these rules, and one draw needn't show every extreme that they name: `points`: channels 0 and 1 are plate positions, channel 2 is a positive film gap. `skeleton`: each node's 128 entries are distinct. `owner_map`: among the 16 nodes of one device, at most 2 have the same owner, and exactly 2 do for some owner. `coupling`: each 128-row block is symmetric and its diagonal exceeds the sum of the other magnitudes of its row by 0.5 or more.
All inputs are finite; a program needn't handle non-finite values.
Results may differ from the reference program's by a relative error of at most 0.0003.
Values sent between devices are 32-bit elements; how exact they have to be, the bound alone decides.
A program may use at most 128 MiB of HBM per device.

```python
import math
import jax
import jax.numpy as jnp
import numpy as np
from jax import lax

LEAF = 512
K = 128
NEAR = 2
CAP = 2
NODES = 16
LEVELS = 8
NODES_ALL = 512
N_ROW = 32


def draw_points(key, part):
    key = jax.random.fold_in(key, 11)
    place_key, gap_key = jax.random.split(key)
    spots = jax.random.uniform(place_key, (LEVELS, NODES_ALL, 2, LEAF), jnp.float32, 0.5, 4.5)
    gap_low, gap_high = (0.05, 0.5)
    gaps = jnp.exp(jax.random.uniform(gap_key, (LEVELS, NODES_ALL, 1, LEAF), jnp.float32, math.log(gap_low), math.log(gap_high)))
    return jnp.concatenate([spots, gaps], axis=2)


def draw_skeleton(key, part):
    key = jax.random.fold_in(key, 12)
    noise = jax.random.randint(key, (LEVELS, NODES_ALL, LEAF), 0, 2 ** 20, jnp.int32)
    row_iota = lax.broadcasted_iota(jnp.int32, (LEVELS, NODES_ALL, LEAF), 2)
    node_iota = lax.broadcasted_iota(jnp.int32, (LEVELS, NODES_ALL, LEAF), 1)
    scores = noise * LEAF + row_iota
    scores = jnp.where((node_iota == 0) & (row_iota == LEAF - 1), -1, scores)
    scores = jnp.where((node_iota == 0) & (row_iota == 0), -2, scores)
    ordering = jnp.argsort(scores, axis=-1, stable=True)
    return ordering[..., :K].astype(jnp.int32)


def draw_coupling(key, part):
    key = jax.random.fold_in(key, 13)
    off_key, diag_key = jax.random.split(key)
    raw_values = jax.random.uniform(off_key, (LEVELS, N_ROW, K, K), jnp.float32, -1.0, 1.0)
    symmetric = (raw_values + jnp.swapaxes(raw_values, 2, 3)) * (0.75 / K)
    diag_high = 4.0
    diagonal = jax.random.uniform(diag_key, (LEVELS, N_ROW, K, 1), jnp.float32, 2.0, diag_high)
    eye_mask = lax.broadcasted_iota(jnp.int32, (K, K), 0) == lax.broadcasted_iota(jnp.int32, (K, K), 1)
    blocks = jnp.where(eye_mask, diagonal, symmetric)
    return blocks.reshape(LEVELS, N_ROW * K, K)


def with_ends(entries, rng, smallest, top_value):
    dims = entries.shape
    spot = [jax.random.randint(jax.random.fold_in(rng, axis), (), 0, dims[axis]) for axis in range(len(dims))]
    entries = entries.at[tuple(spot)].set(smallest)
    longest = dims.index(max(dims))
    spot[longest] = (spot[longest] + 1) % dims[longest]
    return entries.at[tuple(spot)].set(top_value)


def block_levels(rng, extent, shards, least, high):
    factor_of, own = 1.0, jax.random.fold_in(rng, 6)
    for axis_at, blocks in shards:
        heights = jnp.exp(jax.random.uniform(jax.random.fold_in(own, axis_at), (blocks,), jnp.float32, least / len(shards), high / len(shards)))
        factor_of = factor_of * jnp.repeat(heights, extent[axis_at] // blocks).reshape([-1 if axis == axis_at else 1 for axis in range(len(extent))])
    return factor_of


def assign_block(stream_key, own, number, rows, count, top, limit, slope):
    sequence = jax.random.permutation(stream_key, count)
    crowded, ordinary = shares(count, rows * top, limit, slope, True), shares(count, rows * top, limit, slope, False)
    places = jnp.arange(count)

    def named(sizes, rotation):
        used = int((sizes > 0).sum())
        fixed = max(1, used // 4)
        moved = fixed + (places - fixed + rotation * (used - fixed)) % max(1, count - fixed)
        return jnp.zeros((count,), jnp.int32).at[sequence[jnp.where(places < fixed, places, moved)]].set(jnp.asarray(sizes, jnp.int32))

    sizes = jnp.where(number % 4 == 0, named(crowded, number // 4), named(ordinary, number - number // 4 - 1))
    mixed = jax.random.permutation(jax.random.fold_in(own, 3), count)
    source_of, taker = mixed[0:count // 2 * 2:2], mixed[1:count // 2 * 2:2]
    room = jnp.minimum(sizes[source_of] - 1, limit - sizes[taker]) // 2
    room = jnp.where((source_of == sequence[0]) | (taker == sequence[0]) | (sizes[taker] == 0), 0, jnp.maximum(room, 0))
    moved = jax.random.randint(jax.random.fold_in(own, 4), (count // 2,), 0, 1 << 20) % (room + 1)
    sizes = sizes.at[source_of].add(-moved).at[taker].add(moved)
    items = jnp.searchsorted(jnp.cumsum(sizes), jnp.arange(rows * top), side="right").astype(jnp.int32)
    listing = items.reshape(top, rows).T
    listing = listing[jax.random.permutation(jax.random.fold_in(own, 1), rows)]
    rotation = jax.random.randint(jax.random.fold_in(own, 2), (rows, 1), 0, top)
    return jnp.take_along_axis(listing, (jnp.arange(top)[None, :] + rotation) % top, axis=1)


def shares(amount, total, limit, slope, full):
    loads = [(1 << 20) // math.isqrt(grade ** slope) + 1 for grade in range(1, amount + 1)]
    largest = limit if full else min(limit, max(-(-total // amount), total * loads[0] // sum(loads)))
    least = 1 if total - largest >= amount - 1 else 0
    given, surplus = [largest] + [least] * (amount - 1), total - largest - least * (amount - 1)
    while surplus > 0:
        candidates = [i for i in range(1, amount) if given[i] < largest] or [i for i in range(1, amount) if given[i] < limit]
        mass, budget = sum([loads[i] for i in candidates]), surplus
        for i in candidates:
            addition = min(limit - given[i], max(1, budget * loads[i] // mass), surplus)
            given[i] = given[i] + addition
            surplus = surplus - addition
    return np.array(given)


def bell_draw(key, dims, scale, most, pieces=(), held_as=jnp.bfloat16):
    factor_of = block_levels(key, dims, pieces, -0.22, 0.18) if pieces else 1.0
    drawn = jax.random.normal(key, dims, jnp.float32) * scale * factor_of
    return jnp.minimum(jnp.maximum(drawn, -most), most).astype(held_as)


def setup_inputs(seed: int = 0) -> dict:
    keys = jax.random.split(jax.random.key(seed), 8)
    points = draw_points(jax.random.fold_in(keys[7], 71), 0)
    panels = bell_draw(keys[1], (LEVELS, NODES_ALL, LEAF, K), 1.0, 6.0, ((0, 8), (1, 32)), jnp.float32)
    near_nodes = with_ends(jax.random.randint(keys[2], (LEVELS, NODES_ALL, NEAR), 0, 3 * NODES), jax.random.fold_in(keys[2], 1), 0, (3 * NODES) - 1).astype(jnp.int32)
    skeleton = draw_skeleton(jax.random.fold_in(keys[7], 71), 0)
    owner_map_keys = jax.random.split(jax.random.fold_in(keys[4], 1), LEVELS * NODES_ALL // NODES)
    owner_map_turns = jax.random.permutation(jax.random.fold_in(keys[4], 3), LEVELS * NODES_ALL // NODES)
    owner_map = jax.vmap(lambda own, number: assign_block(jax.random.fold_in(keys[4], 2), own, number, NODES, N_ROW, 1, CAP, 2))(owner_map_keys, owner_map_turns).reshape((LEVELS, NODES_ALL, 1))
    transfer = bell_draw(keys[5], (LEVELS, NODES_ALL, K, K), (2 * K) ** -0.5, 0.375, ((0, 8), (1, 32)), jnp.float32)
    coupling = draw_coupling(jax.random.fold_in(keys[7], 71), 0)
    return {"points": points, "panels": panels, "near_nodes": near_nodes, "skeleton": skeleton, "owner_map": owner_map, "transfer": transfer, "coupling": coupling}


highest = lax.Precision.HIGHEST

def kernel_block(own_points, far_points):
    delta_x = own_points[0][:, None] - far_points[0][None, :]
    delta_y = own_points[1][:, None] - far_points[1][None, :]
    gaps = own_points[2][:, None] * far_points[2][None, :]
    return lax.rsqrt(delta_x * delta_x + delta_y * delta_y + gaps) * own_points.shape[1] ** (-0.5)

def factor(coupled, carried):
    gram_term = jnp.dot(carried.T, carried, precision=highest) / carried.shape[1]
    factor_low = jnp.linalg.cholesky(coupled + gram_term)
    return lax.linalg.triangular_solve(factor_low, carried.T, left_side=True, lower=True).T

def level_blocks(inputs_level):
    level_points, level_panels, level_near, level_rows = inputs_level

    def one_node(global_node):
        own_points = level_points[global_node]
        result = jnp.dot(kernel_block(own_points, own_points), level_panels[global_node], precision=highest)
        for near_slot in range(NEAR):
            target = global_node // NODES * NODES + level_near[global_node, near_slot] - NODES
            inside = (target >= 0) & (target < NODES_ALL)
            clipped = jnp.clip(target, 0, NODES_ALL - 1).astype(jnp.int32)
            contrib = jnp.dot(kernel_block(own_points, level_points[clipped]), level_panels[clipped], precision=highest)
            result = result + jnp.where(inside, contrib, jnp.zeros_like(contrib))
        return jnp.take(result, level_rows[global_node], axis=0)
    return lax.map(one_node, jnp.arange(NODES_ALL, dtype=jnp.int32))

def reference(points, panels, near_nodes, skeleton, owner_map, transfer, coupling):
    local_block = lax.map(level_blocks, (points, panels, near_nodes, skeleton))

    def climb(carried, inputs_level):
        level_transfer, level_local = inputs_level
        carried = jnp.einsum('nab,nbc->nac', level_transfer, carried, precision=highest) + level_local
        return (carried, carried)
    start = jnp.zeros((NODES_ALL, K, K), jnp.float32)
    unused, carried_all = lax.scan(climb, start, (transfer, local_block))
    owners_blocks = coupling.reshape(LEVELS, N_ROW, K, K)

    def level_factor(inputs_level):
        level_coupling, level_owner, level_carried = inputs_level
        chosen = jnp.take(level_coupling, level_owner[:, 0], axis=0)
        return jax.vmap(factor)(chosen, level_carried)
    return lax.map(level_factor, (owners_blocks, owner_map, carried_all))
```

```python
import jax
import jax.numpy as jnp
from jax import lax
from jax.experimental import pallas as pl
from jax.experimental.pallas import tpu as pltpu
from jax.sharding import PartitionSpec as P
F32, BF16 = jnp.float32, jnp.bfloat16
NN, R, W = 16, 128, 32

def halves(x):
    high = x.astype(BF16)
    return high, (x - high.astype(F32)).astype(BF16)

def dot(a, b, dims=((1,), (0,))):
    return lax.dot_general(a, b, (dims, ((), ())), preferred_element_type=F32)

def spread_row(x, row):
    return jnp.broadcast_to(x[row:row + 1, :], x.shape)

def lane_pick(x, index):
    return jnp.take_along_axis(x, index, axis=1)

def invert_factors(diag, step):
    groups, parts = len(diag), W // 8
    lane = lax.broadcasted_iota(jnp.int32, (8, R), 1)
    row = lax.broadcasted_iota(jnp.int32, (8, R), 0)
    seg = (lane // W) * W
    within = lane % W
    rest = [list(d) for d in diag]
    work = [[jnp.where(within == row + 8 * q, 1.0, 0.0).astype(F32) for q in range(parts)] for _ in range(groups)]
    done = [[jnp.zeros((8, R), F32) for q in range(parts)] for _ in range(groups)]
    for j in range(0, W, step):
        q0 = j // 8
        for g in range(groups):
            cols = [{q: lane_pick(rest[g][q], seg + (j + t)) for q in range(q0, parts)} for t in range(step)]
            rows = [spread_row(rest[g][q0], (j + t) % 8) for t in range(step)]
            wrows = [spread_row(work[g][q0], (j + t) % 8) for t in range(step)]
            for t in range(step):
                at = (j + t) % 8
                scale = lax.rsqrt(spread_row(cols[t][q0], at))
                left = {q: cols[t][q] * scale for q in range(q0, parts)}
                right = rows[t] * scale
                wright = wrows[t] * scale
                for u in range(t + 1, step):
                    f = spread_row(left[q0], (j + u) % 8)
                    rows[u] = rows[u] - f * right
                    wrows[u] = wrows[u] - f * wright
                    for q in range(q0, parts):
                        cols[u][q] = cols[u][q] - left[q] * f
                done[g][q0] = jnp.where(row == at, wright, done[g][q0])
                for q in range(q0, parts):
                    l = jnp.where(row > at, left[q], 0.0) if q == q0 else left[q]
                    rest[g][q] = rest[g][q] - l * right
                    work[g][q] = work[g][q] - l * wright
    return done

def eliminate_kernel(step, owner_ref, c_ref, s_ref, out_ref, hw):
    rows128 = lax.broadcasted_iota(jnp.int32, (R, R), 0)
    lanes128 = lax.broadcasted_iota(jnp.int32, (R, R), 1)
    eye = jnp.where(rows128 == lanes128, 1.0, 0.0).astype(F32)
    for n in range(NN):
        ch, cl = halves(c_ref[n])
        gram = dot(jnp.concatenate([ch, ch, cl], 0), jnp.concatenate([ch, cl, ch], 0), ((0,), (0,)))
        s = s_ref[owner_ref[n]]
        hw[n, :, 0:R] = s + gram * (1.0 / R)
        hw[n, :, R:2 * R] = eye
    lane32 = lax.broadcasted_iota(jnp.int32, (W, R), 1) // W
    per = R // W
    groups = NN // per
    for k in range(per):
        r0 = W * k
        diag = []
        for g in range(groups):
            packed = None
            for t in range(per):
                x = hw[per * g + t, r0:r0 + W, 0:R]
                if t != k:
                    x = pltpu.roll(x, (W * (t - k)) % R, 1)
                packed = x if packed is None else jnp.where(lane32 == t, x, packed)
            diag.append([packed[8 * q:8 * q + 8] for q in range(W // 8)])
        inv = invert_factors(diag, step)
        for g in range(groups):
            m = jnp.concatenate(inv[g], axis=0)
            md = jnp.concatenate([jnp.where(lane32 == t, m, 0.0) for t in range(per)], axis=0)
            mh, ml = halves(md)
            x = jnp.concatenate([hw[per * g + t, r0:r0 + W, :] for t in range(per)], axis=0)
            xh, xl = halves(x)
            x = dot(mh, xh) + (dot(mh, xl) + dot(ml, xh))
            xh, xl = halves(x)
            for t in range(per):
                n = per * g + t
                lo = slice(W * t, W * t + W)
                hw[n, r0:r0 + W, R:2 * R] = x[lo, R:]
                if k < per - 1:
                    lhs = jnp.concatenate([xh[lo, :R], xh[lo, :R], xl[lo, :R]], axis=0)
                    rhs = jnp.concatenate([xh[lo], xl[lo], xh[lo]], axis=0)
                    upd = dot(lhs, rhs, ((0,), (0,)))
                    hw[n, r0 + W:, :] = hw[n, r0 + W:, :] - upd[r0 + W:, :]
    for n in range(NN):
        ch, cl = halves(c_ref[n])
        wh, wl = halves(hw[n, :, R:2 * R])
        both = dot(jnp.concatenate([ch, ch], 1), jnp.concatenate([wh, wl], 1), ((1,), (1,)))
        out_ref[n] = both + dot(cl, wh, ((1,), (1,)))


def eliminate(owner, c, s, step=4):
    vm = pl.BlockSpec(memory_space=pltpu.VMEM)
    sm = pl.BlockSpec(memory_space=pltpu.SMEM)
    return pl.pallas_call(
        lambda *r: eliminate_kernel(step, *r),
        out_shape=jax.ShapeDtypeStruct((NN, R, R), F32),
        in_specs=[sm, vm, vm],
        out_specs=vm,
        scratch_shapes=[pltpu.VMEM((NN, R, 2 * R), F32)],
        compiler_params=pltpu.CompilerParams(vmem_limit_bytes=40 << 20),
        name="eliminate",
    )(owner, c, s)
LEAF = 512

def skeleton_columns(points_ref, skeleton_ref, columns, base, count):
    for n0 in range(0, count, 8):
        at = skeleton_ref[n0:n0 + 8, :]
        inside, tile = at % R, at // R
        for c in range(3):
            got = None
            for t in range(LEAF // R):
                part = points_ref[n0:n0 + 8, c, t * R:(t + 1) * R]
                part = jnp.take_along_axis(part, inside, axis=1)
                got = part if got is None else jnp.where(tile == t, part, got)
            turned = got.T
            for n in range(8):
                columns[base + n0 + n, c] = jnp.broadcast_to(turned[:, n:n + 1], (R, R))

def one_block(columns, points_ref, panels_ref, node, far):
    pairs = []
    near_x, near_y, near_g = columns[node, 0], columns[node, 1], columns[node, 2]
    total = None
    for h in range(2):
        parts = []
        for t in range(2):
            lanes = slice((2 * h + t) * R, (2 * h + t + 1) * R)
            dx = near_x - points_ref[far, 0:1, lanes]
            dy = near_y - points_ref[far, 1:2, lanes]
            parts.append(lax.rsqrt(dx * dx + dy * dy + near_g * points_ref[far, 2:3, lanes]))
        kh, kl = halves(jnp.concatenate(parts, axis=1))
        ph, pl_ = halves(panels_ref[far, 2 * h * R:(2 * h + 2) * R, :])
        both = dot(kh, jnp.concatenate([ph, pl_], axis=1))
        part = both[:, :R] + both[:, R:] + dot(kl, ph)
        total = part if total is None else total + part
    return total * LEAF ** (-0.5)

def near_list(near_ref, todo, spans, start):
    count = start
    for base, low, high in spans:
        def visit(i, count):
            node, slot = base + i // 2, i % 2
            place = near_ref[node, slot]
            inside = (place >= low) & (place < high)
            todo[count] = node * NN + jnp.where(inside, place - low, 0)
            return count + inside.astype(jnp.int32)
        count = lax.fori_loop(0, 2 * NN, visit, count)
    return count

def run_list(todo, count, spare, unroll, columns, points_ref, panels_ref, total):
    for u in range(unroll - 1):
        todo[count + u] = spare * NN
    def body(i, carry):
        got = []
        for u in range(unroll):
            entry = todo[unroll * i + u]
            got.append((entry // NN, one_block(columns, points_ref, panels_ref, entry // NN, entry % NN)))
        for node, block in got:
            total[node] = total[node] + block
        return carry
    lax.fori_loop(0, (count + unroll - 1) // unroll, body, 0)

def lent_kernel(unroll, near_ref, points_ref, panels_ref, far_points, far_skeleton, out_ref, columns, total, todo, edges):
    first, last = edges()
    for side in range(2):
        skeleton_columns(far_points.at[side], far_skeleton.at[side], columns, side * NN, NN)
    columns[2 * NN] = jnp.ones_like(columns[2 * NN])
    total[...] = jnp.zeros_like(total)
    spans = ((0, 32, jnp.where(first, 0, 48)), (NN, 0, jnp.where(last, 0, 16)))
    count = near_list(near_ref, todo, spans, 0)
    run_list(todo, count, 2 * NN, unroll, columns, points_ref, panels_ref, total)
    out_ref[...] = total[0:2 * NN].reshape(out_ref.shape)

def own_kernel(unroll, near_ref, points_ref, panels_ref, skeleton_ref, out_ref, columns, total, todo):
    skeleton_columns(points_ref, skeleton_ref, columns, 0, NN)
    columns[NN] = jnp.ones_like(columns[NN])
    total[...] = jnp.zeros_like(total)
    def visit(i, c):
        todo[i] = i * NN + i
        return c
    lax.fori_loop(0, NN, visit, 0)
    count = near_list(near_ref, todo, ((0, 16, 32),), NN)
    run_list(todo, count, NN, unroll, columns, points_ref, panels_ref, total)
    out_ref[...] = total[0:NN]

vm = pl.BlockSpec(memory_space=pltpu.VMEM)
sm = pl.BlockSpec(memory_space=pltpu.SMEM)
def lent(near, points, panels, far_points, far_skeleton, edges, unroll=2):
    return pl.pallas_call(lambda *r: lent_kernel(unroll, *r, edges),
        out_shape=jax.ShapeDtypeStruct((2, NN, R, R), F32), in_specs=[sm, vm, vm, vm, vm], out_specs=vm,
        scratch_shapes=[pltpu.VMEM((2 * NN + 1, 3, R, R), F32), pltpu.VMEM((2 * NN + 1, R, R), F32), pltpu.SMEM((80,), jnp.int32)],
        compiler_params=pltpu.CompilerParams(vmem_limit_bytes=40 << 20), name="lent")(near, points, panels, far_points, far_skeleton)
def own(near, points, panels, skeleton, unroll=2):
    return pl.pallas_call(lambda *r: own_kernel(unroll, *r),
        out_shape=jax.ShapeDtypeStruct((NN, R, R), F32), in_specs=[sm, vm, vm, vm], out_specs=vm,
        scratch_shapes=[pltpu.VMEM((NN + 1, 3, R, R), F32), pltpu.VMEM((NN + 1, R, R), F32), pltpu.SMEM((64,), jnp.int32)],
        compiler_params=pltpu.CompilerParams(vmem_limit_bytes=40 << 20), name="own")(near, points, panels, skeleton)


def edges():
    row = lax.axis_index("row")
    return row == 0, row == lax.axis_size("row") - 1


def moved(array, axis, distance):
    count = lax.axis_size(axis)
    return lax.ppermute(array, axis, [(i, (i + distance) % count) for i in range(count)])


def per_device(points, panels, near_nodes, skeleton, owner_map, transfer, coupling):
    points, panels, near_nodes, skeleton = points[0], panels[0], near_nodes[0], skeleton[0]
    everyone = lax.all_gather(coupling[0].reshape(R, R), "row", axis=0)
    far_points = jnp.stack([moved(points, "row", 1), moved(points, "row", -1)])
    far_skeleton = jnp.stack([moved(skeleton, "row", 1), moved(skeleton, "row", -1)])
    far_near = jnp.concatenate([moved(near_nodes, "row", 1), moved(near_nodes, "row", -1)])
    sums = lent(far_near, points, panels, far_points, far_skeleton, edges)
    from_next = moved(sums[0], "row", -1)
    from_previous = moved(sums[1], "row", 1)
    local_block = own(near_nodes, points, panels, skeleton) + from_previous + from_next
    carried = local_block
    levels = lax.axis_size("level")
    for _ in range(levels - 1):
        below = lax.ppermute(carried, "level", [(i, i + 1) for i in range(levels - 1)])
        carried = local_block + jnp.einsum(
            "nab,nbc->nac", transfer[0], below, precision=lax.Precision.HIGHEST
        )
    return eliminate(owner_map[0, :, 0], carried, everyone)[None]


def solution(mesh):
    return jax.shard_map(
        per_device,
        mesh=mesh,
        in_specs=(
            P("level", "row", None, None),
            P("level", "row", None, None),
            P("level", "row", None),
            P("level", "row", None),
            P("level", "row", None),
            P("level", "row", None, None),
            P("level", "row", None),
        ),
        out_specs=P("level", "row", None, None),
        check_vma=False,
    )
```

```python
import jax
import jax.numpy as jnp
from jax import lax
from jax.experimental import pallas as pl
from jax.experimental.pallas import tpu as pltpu
from jax.sharding import PartitionSpec as P
F32, BF16 = jnp.float32, jnp.bfloat16
NN, R, W = 16, 128, 32

def halves(x):
    high = x.astype(BF16)
    return high, (x - high.astype(F32)).astype(BF16)

def dot(a, b, dims=((1,), (0,))):
    return lax.dot_general(a, b, (dims, ((), ())), preferred_element_type=F32)

def spread_row(x, row):
    return jnp.broadcast_to(x[row:row + 1, :], x.shape)

def lane_pick(x, index):
    return jnp.take_along_axis(x, index, axis=1)

def invert_factors(diag, step):
    groups, parts = len(diag), W // 8
    lane = lax.broadcasted_iota(jnp.int32, (8, R), 1)
    row = lax.broadcasted_iota(jnp.int32, (8, R), 0)
    seg = (lane // W) * W
    within = lane % W
    rest = [list(d) for d in diag]
    work = [[jnp.where(within == row + 8 * q, 1.0, 0.0).astype(F32) for q in range(parts)] for _ in range(groups)]
    done = [[jnp.zeros((8, R), F32) for q in range(parts)] for _ in range(groups)]
    for j in range(0, W, step):
        q0 = j // 8
        for g in range(groups):
            cols = [{q: lane_pick(rest[g][q], seg + (j + t)) for q in range(q0, parts)} for t in range(step)]
            rows = [spread_row(rest[g][q0], (j + t) % 8) for t in range(step)]
            wrows = [spread_row(work[g][q0], (j + t) % 8) for t in range(step)]
            for t in range(step):
                at = (j + t) % 8
                scale = lax.rsqrt(spread_row(cols[t][q0], at))
                left = {q: cols[t][q] * scale for q in range(q0, parts)}
                right = rows[t] * scale
                wright = wrows[t] * scale
                for u in range(t + 1, step):
                    f = spread_row(left[q0], (j + u) % 8)
                    rows[u] = rows[u] - f * right
                    wrows[u] = wrows[u] - f * wright
                    for q in range(q0, parts):
                        cols[u][q] = cols[u][q] - left[q] * f
                done[g][q0] = jnp.where(row == at, wright, done[g][q0])
                for q in range(q0, parts):
                    l = jnp.where(row > at, left[q], 0.0) if q == q0 else left[q]
                    rest[g][q] = rest[g][q] - l * right
                    work[g][q] = work[g][q] - l * wright
    return done

def eliminate_kernel(step, owner_ref, c_ref, z_ref, x_ref, out_ref, hw):
    rows128 = lax.broadcasted_iota(jnp.int32, (R, R), 0)
    lanes128 = lax.broadcasted_iota(jnp.int32, (R, R), 1)
    eye = jnp.where(rows128 == lanes128, 1.0, 0.0).astype(F32)
    for n in range(NN):
        ch, cl = halves(c_ref[n])
        gram = dot(jnp.concatenate([ch, ch, cl], 0), jnp.concatenate([ch, cl, ch], 0), ((0,), (0,)))
        oz, ox = owner_ref[n] // 4, owner_ref[n] % 4
        s = jnp.concatenate([z_ref[ox, oz], x_ref[oz, ox]], axis=0)
        hw[n, :, 0:R] = s + gram * (1.0 / R)
        hw[n, :, R:2 * R] = eye
    lane32 = lax.broadcasted_iota(jnp.int32, (W, R), 1) // W
    per = R // W
    groups = NN // per
    for k in range(per):
        r0 = W * k
        diag = []
        for g in range(groups):
            packed = None
            for t in range(per):
                x = hw[per * g + t, r0:r0 + W, 0:R]
                if t != k:
                    x = pltpu.roll(x, (W * (t - k)) % R, 1)
                packed = x if packed is None else jnp.where(lane32 == t, x, packed)
            diag.append([packed[8 * q:8 * q + 8] for q in range(W // 8)])
        inv = invert_factors(diag, step)
        for g in range(groups):
            m = jnp.concatenate(inv[g], axis=0)
            md = jnp.concatenate([jnp.where(lane32 == t, m, 0.0) for t in range(per)], axis=0)
            mh, ml = halves(md)
            x = jnp.concatenate([hw[per * g + t, r0:r0 + W, :] for t in range(per)], axis=0)
            xh, xl = halves(x)
            x = dot(mh, xh) + (dot(mh, xl) + dot(ml, xh))
            xh, xl = halves(x)
            for t in range(per):
                n = per * g + t
                lo = slice(W * t, W * t + W)
                hw[n, r0:r0 + W, R:2 * R] = x[lo, R:]
                if k < per - 1:
                    lhs = jnp.concatenate([xh[lo, :R], xh[lo, :R], xl[lo, :R]], axis=0)
                    rhs = jnp.concatenate([xh[lo], xl[lo], xh[lo]], axis=0)
                    upd = dot(lhs, rhs, ((0,), (0,)))
                    hw[n, r0 + W:, :] = hw[n, r0 + W:, :] - upd[r0 + W:, :]
    for n in range(NN):
        ch, cl = halves(c_ref[n])
        wh, wl = halves(hw[n, :, R:2 * R])
        both = dot(jnp.concatenate([ch, ch], 1), jnp.concatenate([wh, wl], 1), ((1,), (1,)))
        out_ref[n] = both + dot(cl, wh, ((1,), (1,)))


def eliminate(owner, c, by_z, by_x, step=4):
    return pl.pallas_call(
        lambda *r: eliminate_kernel(step, *r),
        out_shape=jax.ShapeDtypeStruct((NN, R, R), F32),
        in_specs=[sm, vm, vm, vm],
        out_specs=vm,
        scratch_shapes=[pltpu.VMEM((NN, R, 2 * R), F32)],
        compiler_params=pltpu.CompilerParams(vmem_limit_bytes=40 << 20),
        name="eliminate",
    )(owner, c, by_z, by_x)
LEAF = 512

def skeleton_columns(points_ref, skeleton_ref, columns, base, count):
    for n0 in range(0, count, 8):
        at = skeleton_ref[n0:n0 + 8, :]
        inside, tile = at % R, at // R
        for c in range(3):
            got = None
            for t in range(LEAF // R):
                part = points_ref[n0:n0 + 8, c, t * R:(t + 1) * R]
                part = jnp.take_along_axis(part, inside, axis=1)
                got = part if got is None else jnp.where(tile == t, part, got)
            turned = got.T
            for n in range(8):
                columns[base + n0 + n, c] = jnp.broadcast_to(turned[:, n:n + 1], (R, R))

def one_block(columns, points_ref, panels_ref, node, far):
    near_x, near_y, near_g = columns[node, 0], columns[node, 1], columns[node, 2]
    total = None
    for h in range(2):
        parts = []
        for t in range(2):
            lanes = slice((2 * h + t) * R, (2 * h + t + 1) * R)
            dx = near_x - points_ref[far, 0:1, lanes]
            dy = near_y - points_ref[far, 1:2, lanes]
            parts.append(lax.rsqrt(dx * dx + dy * dy + near_g * points_ref[far, 2:3, lanes]))
        kh, kl = halves(jnp.concatenate(parts, axis=1))
        ph, pl_ = halves(panels_ref[far, 2 * h * R:(2 * h + 2) * R, :])
        part = dot(jnp.concatenate([kh, kl], axis=0), jnp.concatenate([ph, pl_], axis=1))
        total = part if total is None else total + part
    return (total[:R, :R] + (total[:R, R:] + total[R:, :R])) * LEAF ** (-0.5)

def near_list(near_ref, todo, spans, start):
    count = start
    for base, low, high in spans:
        def visit(i, count):
            node, slot = base + i // 2, i % 2
            place = near_ref[node, slot]
            inside = (place >= low) & (place < high)
            todo[count] = node * NN + jnp.where(inside, place - low, 0)
            return count + inside.astype(jnp.int32)
        count = lax.fori_loop(0, 2 * NN, visit, count)
    return count

def run_list(todo, count, spare, unroll, columns, points_ref, panels_ref, total):
    for u in range(unroll - 1):
        todo[count + u] = spare * NN
    def body(i, carry):
        got = []
        for u in range(unroll):
            entry = todo[unroll * i + u]
            got.append((entry // NN, one_block(columns, points_ref, panels_ref, entry // NN, entry % NN)))
        for node, block in got:
            total[node] = total[node] + block
        return carry
    lax.fori_loop(0, (count + unroll - 1) // unroll, body, 0)

def lent_kernel(unroll, near_ref, points_ref, panels_ref, far_points, far_skeleton, out_ref, columns, total, todo, edges):
    first, last = edges()
    for side in range(2):
        skeleton_columns(far_points.at[side], far_skeleton.at[side], columns, side * NN, NN)
    columns[2 * NN] = jnp.ones_like(columns[2 * NN])
    total[...] = jnp.zeros_like(total)
    spans = ((0, 32, jnp.where(first, 0, 48)), (NN, 0, jnp.where(last, 0, 16)))
    count = near_list(near_ref, todo, spans, 0)
    run_list(todo, count, 2 * NN, unroll, columns, points_ref, panels_ref, total)
    out_ref[...] = total[0:2 * NN].reshape(out_ref.shape)

def own_kernel(unroll, near_ref, points_ref, panels_ref, skeleton_ref, out_ref, columns, total, todo):
    skeleton_columns(points_ref, skeleton_ref, columns, 0, NN)
    columns[NN] = jnp.ones_like(columns[NN])
    total[...] = jnp.zeros_like(total)
    def visit(i, c):
        todo[i] = i * NN + i
        return c
    lax.fori_loop(0, NN, visit, 0)
    count = near_list(near_ref, todo, ((0, 16, 32),), NN)
    run_list(todo, count, NN, unroll, columns, points_ref, panels_ref, total)
    out_ref[...] = total[0:NN]

vm = pl.BlockSpec(memory_space=pltpu.VMEM)
sm = pl.BlockSpec(memory_space=pltpu.SMEM)
def lent(near, points, panels, far_points, far_skeleton, edges, unroll=2):
    return pl.pallas_call(lambda *r: lent_kernel(unroll, *r, edges),
        out_shape=jax.ShapeDtypeStruct((2, NN, R, R), F32), in_specs=[sm, vm, vm, vm, vm], out_specs=vm,
        scratch_shapes=[pltpu.VMEM((2 * NN + 1, 3, R, R), F32), pltpu.VMEM((2 * NN + 1, R, R), F32), pltpu.SMEM((80,), jnp.int32)],
        compiler_params=pltpu.CompilerParams(vmem_limit_bytes=40 << 20), name="lent")(near, points, panels, far_points, far_skeleton)
def own(near, points, panels, skeleton, unroll=2):
    return pl.pallas_call(lambda *r: own_kernel(unroll, *r),
        out_shape=jax.ShapeDtypeStruct((NN, R, R), F32), in_specs=[sm, vm, vm, vm], out_specs=vm,
        scratch_shapes=[pltpu.VMEM((NN + 1, 3, R, R), F32), pltpu.VMEM((NN + 1, R, R), F32), pltpu.SMEM((64,), jnp.int32)],
        compiler_params=pltpu.CompilerParams(vmem_limit_bytes=40 << 20), name="own")(near, points, panels, skeleton)


MESH = pl.DeviceIdType.MESH
NX, NZ, HALF, GS = 4, 8, 64, 2
GROUPS = NN // GS


def places():
    me = lax.axis_index("row")
    count = NX * NZ
    z, x = me // NX, me % NX
    previous, following = (me + count - 1) % count, (me + 1) % count
    along_z = [(z + d) % NZ * NX + x for d in range(1, NZ)]
    along_x = [z * NX + (x + d) % NX for d in range(1, NX)]
    return z, x, previous, following, along_z, along_x


def greet(rows, levels=()):
    barrier = pltpu.get_barrier_semaphore()
    level, row = lax.axis_index("level"), lax.axis_index("row")
    for device in [(level, r) for r in rows] + [(l, row) for l in levels]:
        pl.semaphore_signal(barrier, inc=1, device_id=device, device_id_type=MESH)
    pl.semaphore_wait(barrier, len(rows) + len(levels))


def to_row(source, target, send, recv, row):
    return pltpu.make_async_remote_copy(
        src_ref=source, dst_ref=target, send_sem=send, recv_sem=recv,
        device_id=(lax.axis_index("level"), row), device_id_type=MESH,
    )


def exchange_kernel(points_any, skeleton_any, near_any, coupling, panels_any, points_ref, skeleton_ref,
                    far_points, far_skeleton, far_near, by_z, by_x, self_ref,
                    columns, panels, sends, receives, z_sends, z_receives, x_sends, x_receives, local):
    z, x, previous, following, along_z, along_x = places()
    fetch = pltpu.make_async_copy(panels_any, panels, local.at[0])
    fetch.start()
    keep_z = pltpu.make_async_copy(coupling.at[0:HALF], by_z.at[z], local.at[1])
    keep_x = pltpu.make_async_copy(coupling.at[HALF:R], by_x.at[x], local.at[2])
    keep_z.start()
    keep_x.start()
    greet([previous, following] + along_z + along_x)
    copies = []
    for i, (source, target) in enumerate(((points_any, far_points), (skeleton_any, far_skeleton), (near_any, far_near))):
        copies.append(to_row(source, target.at[0], sends.at[0, i], receives.at[0, i], following))
        copies.append(to_row(source, target.at[1], sends.at[1, i], receives.at[1, i], previous))
    for i, r in enumerate(along_x):
        copies.append(to_row(coupling.at[HALF:R], by_x.at[x], x_sends.at[i], x_receives.at[i], r))
    for i, r in enumerate(along_z):
        copies.append(to_row(coupling.at[0:HALF], by_z.at[z], z_sends.at[i], z_receives.at[i], r))
    for copy in copies:
        copy.start()
    skeleton_columns(points_ref, skeleton_ref, columns, 0, NN)
    fetch.wait()

    def visit(i, carry):
        for u in range(2):
            self_ref[2 * i + u] = one_block(columns, points_ref, panels, 2 * i + u, 2 * i + u)
        return carry

    lax.fori_loop(0, NN // 2, visit, 0)
    keep_z.wait()
    keep_x.wait()
    for copy in copies:
        copy.wait()


def exchange(points, skeleton, near, coupling, panels):
    hbm = pl.BlockSpec(memory_space=pl.ANY)
    shape = jax.ShapeDtypeStruct
    dma = pltpu.SemaphoreType.DMA
    return pl.pallas_call(
        exchange_kernel,
        out_shape=(
            shape((2,) + points.shape, F32), shape((2,) + skeleton.shape, jnp.int32), shape((2,) + near.shape, jnp.int32),
            shape((NZ, HALF, R), F32), shape((NX, HALF, R), F32), shape((NN, R, R), F32),
        ),
        in_specs=[hbm] * 5 + [vm, vm],
        out_specs=(hbm,) * 5 + (vm,),
        scratch_shapes=[
            pltpu.VMEM((NN, 3, R, R), F32), pltpu.VMEM(panels.shape, F32),
            dma((2, 3)), dma((2, 3)), dma((NZ - 1,)), dma((NZ - 1,)), dma((NX - 1,)), dma((NX - 1,)), dma((3,)),
        ],
        compiler_params=pltpu.CompilerParams(collective_id=0, has_side_effects=True, vmem_limit_bytes=24 << 20),
        name="exchange",
    )(points, skeleton, near, coupling, panels, points, skeleton)


def climb_kernel(near_ref, points_ref, panels_ref, skeleton_ref, self_ref, lent_ref, transfer_ref, by_z, by_x,
                 carried, full_z, full_x,
                 columns, wide, lent_in, below, halo_send, halo_receive, up_send, up_receive,
                 z_sends, z_receives, x_sends, x_receives, local):
    z, x, previous, following, along_z, along_x = places()
    level, row = lax.axis_index("level"), lax.axis_index("row")
    top = lax.axis_size("level") - 1
    keep_z = pltpu.make_async_copy(by_z, full_z.at[x], local.at[0])
    keep_x = pltpu.make_async_copy(by_x, full_x.at[z], local.at[1])
    keep_z.start()
    keep_x.start()
    greet([previous, following] + along_z + along_x, [(level + top) % (top + 1), (level + 1) % (top + 1)])

    def halo(g, side):
        part = pl.ds(g * GS, GS)
        return to_row(lent_ref.at[side, part], lent_in.at[side, part], halo_send.at[side, g], halo_receive.at[side, g],
                      following if side else previous)

    def up(g):
        part = pl.ds(g * GS, GS)
        return pltpu.make_async_remote_copy(
            src_ref=carried.at[part], dst_ref=below.at[part], send_sem=up_send.at[g], recv_sem=up_receive.at[g],
            device_id=(level + 1, row), device_id_type=MESH,
        )

    def launch(g, carry):
        halo(g, 0).start()
        halo(g, 1).start()
        return carry

    lax.fori_loop(0, GROUPS, launch, 0)
    spread_x = [to_row(by_x, full_x.at[z], z_sends.at[i], z_receives.at[i], r) for i, r in enumerate(along_z)]
    spread_z = [to_row(by_z, full_z.at[x], x_sends.at[i], x_receives.at[i], r) for i, r in enumerate(along_x)]
    for copy in spread_x:
        copy.start()
    skeleton_columns(points_ref, skeleton_ref, columns, 0, NN)

    def widen(n, carry):
        high, low = halves(transfer_ref[n])
        wide[n] = jnp.concatenate([high, high, low], axis=1)
        return carry

    lax.fori_loop(0, NN, widen, 0)

    def visit(n, carry):
        total = self_ref[n]
        for slot in range(2):
            far = near_ref[n, slot] - NN
            inside = (far >= 0) & (far < NN)
            block = one_block(columns, points_ref, panels_ref, n, jnp.where(inside, far, 0))
            total = total + jnp.where(inside, block, 0.0)
        carried[n] = total
        return carry

    lax.fori_loop(0, NN, visit, 0)
    for copy in spread_z:
        copy.start()

    def climb(g, carry):
        halo(g, 0).wait_recv()
        halo(g, 1).wait_recv()
        for u in range(GS):
            n = g * GS + u
            carried[n] = carried[n] + lent_in[0, n] + lent_in[1, n]

        @pl.when(level > 0)
        def _():
            up(g).wait_recv()
            for u in range(GS):
                n = g * GS + u
                high, low = halves(below[n])
                carried[n] = carried[n] + dot(wide[n], jnp.concatenate([high, low, high], axis=0))

        @pl.when(level < top)
        def _():
            up(g).start()

        return carry

    lax.fori_loop(0, GROUPS, climb, 0)

    def settle(g, carry):
        halo(g, 0).wait_send()
        halo(g, 1).wait_send()

        @pl.when(level < top)
        def _():
            up(g).wait_send()

        return carry

    lax.fori_loop(0, GROUPS, settle, 0)
    keep_z.wait()
    keep_x.wait()
    for copy in spread_x + spread_z:
        copy.wait()


def climb_levels(near, points, panels, skeleton, selves, sums, transfer, by_z, by_x):
    hbm = pl.BlockSpec(memory_space=pl.ANY)
    shape = jax.ShapeDtypeStruct
    dma = pltpu.SemaphoreType.DMA
    return pl.pallas_call(
        climb_kernel,
        out_shape=(shape((NN, R, R), F32), shape((NX, NZ, HALF, R), F32), shape((NZ, NX, HALF, R), F32)),
        in_specs=[sm, vm, vm, vm, vm, vm, vm, hbm, hbm],
        out_specs=(vm, hbm, hbm),
        scratch_shapes=[
            pltpu.VMEM((NN, 3, R, R), F32), pltpu.VMEM((NN, R, 3 * R), BF16),
            pltpu.VMEM((2, NN, R, R), F32), pltpu.VMEM((NN, R, R), F32),
            dma((2, GROUPS)), dma((2, GROUPS)), dma((GROUPS,)), dma((GROUPS,)),
            dma((NZ - 1,)), dma((NZ - 1,)), dma((NX - 1,)), dma((NX - 1,)), dma((2,)),
        ],
        compiler_params=pltpu.CompilerParams(collective_id=1, has_side_effects=True, vmem_limit_bytes=32 << 20),
        name="climb",
    )(near, points, panels, skeleton, selves, sums, transfer, by_z, by_x)


def edges():
    row = lax.axis_index("row")
    return row == 0, row == lax.axis_size("row") - 1


def per_device(points, panels, near_nodes, skeleton, owner_map, transfer, coupling):
    points, panels, near_nodes, skeleton = points[0], panels[0], near_nodes[0], skeleton[0]
    far_points, far_skeleton, far_near, by_z, by_x, selves = exchange(points, skeleton, near_nodes, coupling[0], panels)
    sums = lent(far_near.reshape(2 * NN, 2), points, panels, far_points, far_skeleton, edges)
    carried, full_z, full_x = climb_levels(near_nodes, points, panels, skeleton, selves, sums, transfer[0], by_z, by_x)
    return eliminate(owner_map[0, :, 0], carried, full_z, full_x)[None]


def solution(mesh):
    return jax.shard_map(
        per_device,
        mesh=mesh,
        in_specs=(
            P("level", "row", None, None),
            P("level", "row", None, None),
            P("level", "row", None),
            P("level", "row", None),
            P("level", "row", None),
            P("level", "row", None, None),
            P("level", "row", None),
        ),
        out_specs=P("level", "row", None, None),
        check_vma=False,
    )
```

```python
import jax
import jax.numpy as jnp
from jax import lax
from jax.experimental import pallas as pl
from jax.experimental.pallas import tpu as pltpu
from jax.sharding import PartitionSpec as P
F32, BF16 = jnp.float32, jnp.bfloat16
NN, R, W = 16, 128, 32

def halves(x):
    high = x.astype(BF16)
    return high, (x - high.astype(F32)).astype(BF16)

def dot(a, b, dims=((1,), (0,))):
    return lax.dot_general(a, b, (dims, ((), ())), preferred_element_type=F32)

def spread_row(x, row):
    return jnp.broadcast_to(x[row:row + 1, :], x.shape)

def lane_pick(x, index):
    return jnp.take_along_axis(x, index, axis=1)

def invert_factors(diag, step):
    groups, parts = len(diag), W // 8
    lane = lax.broadcasted_iota(jnp.int32, (8, R), 1)
    row = lax.broadcasted_iota(jnp.int32, (8, R), 0)
    seg = (lane // W) * W
    within = lane % W
    rest = [list(d) for d in diag]
    work = [[jnp.where(within == row + 8 * q, 1.0, 0.0).astype(F32) for q in range(parts)] for _ in range(groups)]
    done = [[jnp.zeros((8, R), F32) for q in range(parts)] for _ in range(groups)]
    for j in range(0, W, step):
        q0 = j // 8
        for g in range(groups):
            cols = [{q: lane_pick(rest[g][q], seg + (j + t)) for q in range(q0, parts)} for t in range(step)]
            rows = [spread_row(rest[g][q0], (j + t) % 8) for t in range(step)]
            wrows = [spread_row(work[g][q0], (j + t) % 8) for t in range(step)]
            for t in range(step):
                at = (j + t) % 8
                scale = lax.rsqrt(spread_row(cols[t][q0], at))
                left = {q: cols[t][q] * scale for q in range(q0, parts)}
                right = rows[t] * scale
                wright = wrows[t] * scale
                for u in range(t + 1, step):
                    f = spread_row(left[q0], (j + u) % 8)
                    rows[u] = rows[u] - f * right
                    wrows[u] = wrows[u] - f * wright
                    for q in range(q0, parts):
                        cols[u][q] = cols[u][q] - left[q] * f
                done[g][q0] = jnp.where(row == at, wright, done[g][q0])
                for q in range(q0, parts):
                    l = jnp.where(row > at, left[q], 0.0) if q == q0 else left[q]
                    rest[g][q] = rest[g][q] - l * right
                    work[g][q] = work[g][q] - l * wright
    return done

def packed_coupling(s):
    row = lax.broadcasted_iota(jnp.int32, (64, R), 0)
    lane = lax.broadcasted_iota(jnp.int32, (64, R), 1)
    low, high = s[64:R, :], s[0:64, :]
    turned = pltpu.roll(high, 64, 1)
    body = jnp.where(lane - 64 > row, turned, jnp.where(lane - 64 == row, 0.5 * low, low))
    diagonal = jnp.sum(jnp.where(lane == row, 0.5 * high, 0.0), axis=0, keepdims=True)
    return body, jnp.broadcast_to(diagonal, (8, R))


def half_coupling(packed):
    row = lax.broadcasted_iota(jnp.int32, (64, R), 0)
    lane = lax.broadcasted_iota(jnp.int32, (64, R), 1)
    body = packed[0:64, :]
    turned = pltpu.roll(body, 64, 1)
    diagonal = jnp.broadcast_to(packed[64:65, :], (64, R))
    top = jnp.where(lane < 64, jnp.where(lane > row, turned, jnp.where(lane == row, diagonal, 0.0)), 0.0)
    low = jnp.where(lane - 64 <= row, body, 0.0)
    return jnp.concatenate([top, low], axis=0)


def eliminate(step, base, nodes, owner_ref, c_ref, spread, out_ref, hw):
    rows128 = lax.broadcasted_iota(jnp.int32, (R, R), 0)
    lanes128 = lax.broadcasted_iota(jnp.int32, (R, R), 1)
    eye = jnp.where(rows128 == lanes128, 1.0, 0.0).astype(F32)
    for n in range(nodes):
        ch, cl = halves(c_ref[base + n])
        gram = dot(jnp.concatenate([ch, ch, cl], 0), jnp.concatenate([ch, cl, ch], 0), ((0,), (0,)))
        owner = owner_ref[base + n]
        half = half_coupling(spread[owner % 4, owner // 4])
        hw[n, :, 0:R] = half + half.T + gram * (1.0 / R)
        hw[n, :, R:2 * R] = eye
    lane32 = lax.broadcasted_iota(jnp.int32, (W, R), 1) // W
    per = R // W
    groups = nodes // per
    for k in range(per):
        r0 = W * k
        diag = []
        for g in range(groups):
            packed = None
            for t in range(per):
                x = hw[per * g + t, r0:r0 + W, 0:R]
                if t != k:
                    x = pltpu.roll(x, (W * (t - k)) % R, 1)
                packed = x if packed is None else jnp.where(lane32 == t, x, packed)
            diag.append([packed[8 * q:8 * q + 8] for q in range(W // 8)])
        inv = invert_factors(diag, step)
        for g in range(groups):
            m = jnp.concatenate(inv[g], axis=0)
            md = jnp.concatenate([jnp.where(lane32 == t, m, 0.0) for t in range(per)], axis=0)
            mh, ml = halves(md)
            x = jnp.concatenate([hw[per * g + t, r0:r0 + W, :] for t in range(per)], axis=0)
            xh, xl = halves(x)
            x = dot(mh, xh) + (dot(mh, xl) + dot(ml, xh))
            xh, xl = halves(x)
            for t in range(per):
                n = per * g + t
                lo = slice(W * t, W * t + W)
                hw[n, r0:r0 + W, R:2 * R] = x[lo, R:]
                if k < per - 1:
                    lhs = jnp.concatenate([xh[lo, :R], xh[lo, :R], xl[lo, :R]], axis=0)
                    rhs = jnp.concatenate([xh[lo], xl[lo], xh[lo]], axis=0)
                    upd = dot(lhs, rhs, ((0,), (0,)))
                    hw[n, r0 + W:, :] = hw[n, r0 + W:, :] - upd[r0 + W:, :]
    for n in range(nodes):
        ch, cl = halves(c_ref[base + n])
        wh, wl = halves(hw[n, :, R:2 * R])
        both = dot(jnp.concatenate([ch, ch], 1), jnp.concatenate([wh, wl], 1), ((1,), (1,)))
        out_ref[base + n] = both + dot(cl, wh, ((1,), (1,)))


LEAF = 512
vm = pl.BlockSpec(memory_space=pltpu.VMEM)


def skeleton_points(points_ref, skeleton_ref, gathered):
    for n0 in range(0, NN, 8):
        at = skeleton_ref[n0:n0 + 8, :]
        inside, tile = at % R, at // R
        for c in range(3):
            got = None
            for t in range(LEAF // R):
                part = points_ref[c, n0:n0 + 8, t * R:(t + 1) * R]
                part = jnp.take_along_axis(part, inside, axis=1)
                got = part if got is None else jnp.where(tile == t, part, got)
            gathered[c, n0:n0 + 8, :] = got


def skeleton_columns(gathered, columns, base):
    for c in range(3):
        for n0 in range(0, NN, 8):
            turned = gathered[c, n0:n0 + 8, :].T
            for n in range(8):
                columns[base + n0 + n, c] = jnp.broadcast_to(turned[:, n:n + 1], (R, R))


def one_block(columns, rows_ref, split_ref, node, far):
    near_x, near_y, near_g = columns[node, 0], columns[node, 1], columns[node, 2]
    parts = []
    for t in range(LEAF // R):
        lanes = slice(t * R, (t + 1) * R)
        dx = near_x - rows_ref[far, 0:1, lanes]
        dy = near_y - rows_ref[far, 1:2, lanes]
        parts.append(lax.rsqrt(dx * dx + dy * dy + near_g * rows_ref[far, 2:3, lanes]))
    kh, kl = halves(jnp.concatenate(parts, axis=1))
    high = dot(kh, split_ref[far])
    return high[:, :R] + (high[:, R:] + dot(kl, split_ref[far, :, 0:R]))


def chosen_block(columns, rows_ref, split_ref, node, far, allowed):
    inside = (far >= 0) & (far < NN) & allowed
    block = one_block(columns, rows_ref, split_ref, node, jnp.where(inside, far, 0))
    return jnp.where(inside, block, 0.0)


MESH = pl.DeviceIdType.MESH
NX, NZ, PACK, GS = 4, 8, 72, 1
GROUPS = NN // GS
SCALE = LEAF ** (-0.5)


def to_row(source, target, send, recv, row):
    return pltpu.make_async_remote_copy(
        src_ref=source, dst_ref=target, send_sem=send, recv_sem=recv,
        device_id=(lax.axis_index("level"), row), device_id_type=MESH,
    )


def climb_kernel(owner_ref, points_hbm, skeleton_hbm, near_hbm, coupling_hbm, panels_hbm, transfer_hbm,
                 solved,
                 points, rows, skeleton, near, panels, split, transfer, wide, coupling, spread,
                 gathered, far_gathered, far_near_vmem, far_near, columns, lent, lent_in, below, carried, hw,
                 fetch_sem, near_sem, ask_send, ask_receive, halo_send, halo_receive, up_send, up_receive,
                 x_send, x_receive, z_send, z_receive):
    level, me = lax.axis_index("level"), lax.axis_index("row")
    top, count = lax.axis_size("level") - 1, NX * NZ
    z, x = me // NX, me % NX
    previous, following = (me + count - 1) % count, (me + 1) % count
    along_x = [z * NX + (x + d) % NX for d in range(1, NX)]
    along_z = [(z + d) % NZ * NX + x for d in range(1, NZ)]

    fetches = [
        pltpu.make_async_copy(source, target, fetch_sem.at[i])
        for i, (source, target) in enumerate(
            ((points_hbm, points), (skeleton_hbm, skeleton), (near_hbm, near), (coupling_hbm, coupling), (panels_hbm, panels), (transfer_hbm, transfer))
        )
    ]
    for copy in fetches:
        copy.start()

    barrier = pltpu.get_barrier_semaphore()
    peers = [(level, r) for r in [previous, following] + along_z + along_x]
    peers += [((level + top) % (top + 1), me), ((level + 1) % (top + 1), me)]
    for device in peers:
        pl.semaphore_signal(barrier, inc=1, device_id=device, device_id_type=MESH)

    for i in (0, 1, 3):
        fetches[i].wait()
    skeleton_points(points, skeleton, gathered)
    body, diagonal = packed_coupling(coupling[...])
    spread[x, z, 0:64, :] = body
    spread[x, z, 64:PACK, :] = diagonal
    pl.semaphore_wait(barrier, len(peers))

    asks = []
    for i, (source, target) in enumerate(((gathered, far_gathered), (near_hbm, far_near_vmem))):
        asks.append(to_row(source, target.at[0], ask_send.at[0, i], ask_receive.at[0, i], following))
        asks.append(to_row(source, target.at[1], ask_send.at[1, i], ask_receive.at[1, i], previous))
    column = [to_row(spread.at[x, z], spread.at[x, z], z_send.at[i], z_receive.at[i], r) for i, r in enumerate(along_z)]
    plane = [to_row(spread.at[x], spread.at[x], x_send.at[i], x_receive.at[i], r) for i, r in enumerate(along_x)]
    for copy in asks + column:
        copy.start()

    for n in range(NN):
        for c in range(3):
            rows[n, c:c + 1, :] = points[c, n:n + 1, :]
    skeleton_columns(gathered, columns, 2 * NN)
    fetches[2].wait()
    fetches[4].wait()

    def divide(n, carry):
        high, low = halves(panels[n])
        split[n] = jnp.concatenate([high, low], axis=1)
        return carry

    lax.fori_loop(0, NN, divide, 0)

    def own(i, carry):
        for u in range(4):
            n = 4 * i + u
            carried[n] = one_block(columns, rows, split, 2 * NN + n, n)
        return carry

    lax.fori_loop(0, NN // 4, own, 0)

    for copy in asks:
        copy.wait()
    turn = pltpu.make_async_copy(far_near_vmem, far_near, near_sem)
    turn.start()
    skeleton_columns(far_gathered.at[0], columns, 0)
    skeleton_columns(far_gathered.at[1], columns, NN)
    turn.wait()

    def halo(n, side):
        return to_row(lent.at[side, n], lent_in.at[side, n], halo_send.at[side, n], halo_receive.at[side, n],
                      following if side else previous)

    def lend(n, carry):
        for side, offset, allowed in ((0, 2 * NN, me > 0), (1, 0, me < count - 1)):
            total = None
            for slot in range(2):
                block = chosen_block(columns, rows, split, side * NN + n, far_near[side, slot, n] - offset, allowed)
                total = block if total is None else total + block
            lent[side, n] = total * SCALE
        halo(n, 0).start()
        halo(n, 1).start()
        return carry

    lax.fori_loop(0, NN, lend, 0)
    for copy in column:
        copy.wait()
    for copy in plane:
        copy.start()

    def near_own(i, carry):
        for u in range(2):
            n = 2 * i + u
            total = carried[n]
            for slot in range(2):
                total = total + chosen_block(columns, rows, split, 2 * NN + n, near[slot, n] - NN, True)
            carried[n] = total * SCALE
        return carry

    lax.fori_loop(0, NN // 2, near_own, 0)
    fetches[5].wait()

    def widen(n, carry):
        high, low = halves(transfer[n])
        wide[n] = jnp.concatenate([high, high, low], axis=1)
        return carry

    lax.fori_loop(0, NN, widen, 0)

    def up(g):
        part = pl.ds(g * GS, GS)
        return pltpu.make_async_remote_copy(
            src_ref=carried.at[part], dst_ref=below.at[part], send_sem=up_send.at[g], recv_sem=up_receive.at[g],
            device_id=(level + 1, me), device_id_type=MESH,
        )

    def climb(g, carry):
        for u in range(GS):
            n = g * GS + u
            halo(n, 0).wait_recv()
            halo(n, 1).wait_recv()
            carried[n] = carried[n] + lent_in[0, n] + lent_in[1, n]

        @pl.when(level > 0)
        def _():
            up(g).wait_recv()
            for u in range(GS):
                n = g * GS + u
                high, low = halves(below[n])
                carried[n] = carried[n] + dot(wide[n], jnp.concatenate([high, low, high], axis=0))

        @pl.when(level < top)
        def _():
            up(g).start()

        return carry

    lax.fori_loop(0, GROUPS, climb, 0)
    for copy in plane:
        copy.wait()
    eliminate(4, 0, NN, owner_ref, carried, spread, solved, hw)

    def settle(g, carry):
        for u in range(GS):
            halo(g * GS + u, 0).wait_send()
            halo(g * GS + u, 1).wait_send()

        @pl.when(level < top)
        def _():
            up(g).wait_send()

        return carry

    lax.fori_loop(0, GROUPS, settle, 0)


def climb_levels(owner, points, skeleton, near, coupling, panels, transfer):
    hbm = pl.BlockSpec(memory_space=pltpu.HBM)
    shape = jax.ShapeDtypeStruct
    dma = pltpu.SemaphoreType.DMA
    v = pltpu.VMEM
    return pl.pallas_call(
        climb_kernel,
        out_shape=shape((NN, R, R), F32),
        in_specs=[pl.BlockSpec(memory_space=pltpu.SMEM)] + [hbm] * 6,
        out_specs=vm,
        scratch_shapes=[
            v(points.shape, F32), v((NN, 3, LEAF), F32), v(skeleton.shape, jnp.int32), pltpu.SMEM(near.shape, jnp.int32), v(panels.shape, F32),
            v((NN, LEAF, 2 * R), BF16), v((NN, R, R), F32), v((NN, R, 3 * R), BF16), v((R, R), F32), v((NX, NZ, PACK, R), F32),
            v((3, NN, R), F32), v((2, 3, NN, R), F32), v((2,) + near.shape, jnp.int32),
            pltpu.SMEM((2,) + near.shape, jnp.int32), v((3 * NN, 3, R, R), F32),
            v((2, NN, R, R), F32), v((2, NN, R, R), F32), v((NN, R, R), F32),
            v((NN, R, R), F32), v((NN, R, 2 * R), F32),
            dma((6,)), dma, dma((2, 2)), dma((2, 2)), dma((2, NN)), dma((2, NN)), dma((GROUPS,)), dma((GROUPS,)),
            dma((NX - 1,)), dma((NX - 1,)), dma((NZ - 1,)), dma((NZ - 1,)),
        ],
        compiler_params=pltpu.CompilerParams(collective_id=0, has_side_effects=True, vmem_limit_bytes=58 << 20),
        name="climb",
    )(owner, points, skeleton, near, coupling, panels, transfer)


def per_device(points, panels, near_nodes, skeleton, owner_map, transfer, coupling):
    return climb_levels(
        owner_map[0, :, 0], points[0].transpose(1, 0, 2), skeleton[0], near_nodes[0].T, coupling[0], panels[0], transfer[0]
    )[None]


def solution(mesh):
    return jax.shard_map(
        per_device,
        mesh=mesh,
        in_specs=(
            P("level", "row", None, None),
            P("level", "row", None, None),
            P("level", "row", None),
            P("level", "row", None),
            P("level", "row", None),
            P("level", "row", None, None),
            P("level", "row", None),
        ),
        out_specs=P("level", "row", None, None),
        check_vma=False,
    )
```

```python
import jax
import jax.numpy as jnp
from jax import lax
from jax.experimental import pallas as pl
from jax.experimental.pallas import tpu as pltpu
from jax.sharding import PartitionSpec as P
F32, BF16 = jnp.float32, jnp.bfloat16
NN, R, W = 16, 128, 32

def halves(x):
    high = x.astype(BF16)
    return high, (x - high.astype(F32)).astype(BF16)

def dot(a, b, dims=((1,), (0,))):
    return lax.dot_general(a, b, (dims, ((), ())), preferred_element_type=F32)

def spread_row(x, row):
    return jnp.broadcast_to(x[row:row + 1, :], x.shape)

def lane_pick(x, index):
    return jnp.take_along_axis(x, index, axis=1)

def invert_factors(diag, step):
    groups, parts = len(diag), W // 8
    lane = lax.broadcasted_iota(jnp.int32, (8, R), 1)
    row = lax.broadcasted_iota(jnp.int32, (8, R), 0)
    seg = (lane // W) * W
    within = lane % W
    rest = [list(d) for d in diag]
    work = [[jnp.where(within == row + 8 * q, 1.0, 0.0).astype(F32) for q in range(parts)] for _ in range(groups)]
    for j in range(0, W, step):
        q0 = j // 8
        for g in range(groups):
            cols = [{q: lane_pick(rest[g][q], seg + (j + t)) for q in range(q0, parts)} for t in range(step)]
            rows = [spread_row(rest[g][q0], (j + t) % 8) for t in range(step)]
            wrows = [spread_row(work[g][q0], (j + t) % 8) for t in range(step)]
            for t in range(step):
                at = (j + t) % 8
                scale = lax.rsqrt(spread_row(cols[t][q0], at))
                left = {q: cols[t][q] * scale for q in range(q0, parts)}
                right = rows[t] * scale
                wright = wrows[t] * scale
                for u in range(t + 1, step):
                    f = spread_row(left[q0], (j + u) % 8)
                    rows[u] = rows[u] - f * right
                    wrows[u] = wrows[u] - f * wright
                    for q in range(q0, parts):
                        cols[u][q] = cols[u][q] - left[q] * f
                for q in range(q0, parts):
                    l = jnp.where(row > at, left[q], 0.0) if q == q0 else left[q]
                    rest[g][q] = rest[g][q] - l * right
                    work[g][q] = work[g][q] - l * wright
                work[g][q0] = jnp.where(row == at, wright, work[g][q0])
    return work

def packed_coupling(s):
    row = lax.broadcasted_iota(jnp.int32, (64, R), 0)
    lane = lax.broadcasted_iota(jnp.int32, (64, R), 1)
    low, high = s[64:R, :], s[0:64, :]
    turned = pltpu.roll(high, 64, 1)
    body = jnp.where(lane - 64 > row, turned, jnp.where(lane - 64 == row, 0.5 * low, low))
    diagonal = jnp.sum(jnp.where(lane == row, 0.5 * high, 0.0), axis=0, keepdims=True)
    return body, jnp.broadcast_to(diagonal, (8, R))


def half_coupling(packed):
    row = lax.broadcasted_iota(jnp.int32, (64, R), 0)
    lane = lax.broadcasted_iota(jnp.int32, (64, R), 1)
    body = packed[0:64, :]
    turned = pltpu.roll(body, 64, 1)
    diagonal = jnp.broadcast_to(packed[64:65, :], (64, R))
    top = jnp.where(lane < 64, jnp.where(lane > row, turned, jnp.where(lane == row, diagonal, 0.0)), 0.0)
    low = jnp.where(lane - 64 <= row, body, 0.0)
    return jnp.concatenate([top, low], axis=0)


def eliminate(step, base, nodes, owner_ref, c_ref, by_z, by_x, out_ref, hw):
    for n in range(nodes):
        ch, cl = halves(c_ref[base + n])
        gram = dot(jnp.concatenate([ch, ch, cl], 0), jnp.concatenate([ch, cl, ch], 0), ((0,), (0,)))
        owner = owner_ref[base + n]
        half = half_coupling(jnp.concatenate([by_z[owner % 4, owner // 4], by_x[owner // 4, owner % 4]], axis=0))
        hw[n] = half + half.T + gram * (1.0 / R)
    lane = lax.broadcasted_iota(jnp.int32, (W, R), 1)
    row = lax.broadcasted_iota(jnp.int32, (W, R), 0)
    per = R // W
    groups = nodes // per
    for k in range(per):
        r0 = W * k
        diag = []
        for g in range(groups):
            packed = None
            for t in range(per):
                x = hw[per * g + t, r0:r0 + W, :]
                if t != k:
                    x = pltpu.roll(x, (W * (t - k)) % R, 1)
                packed = x if packed is None else jnp.where(lane // W == t, x, packed)
            diag.append([packed[8 * q:8 * q + 8] for q in range(W // 8)])
        inv = invert_factors(diag, step)
        unit = jnp.where(lane - r0 == row, 1.0, 0.0).astype(F32)
        for g in range(groups):
            m = jnp.concatenate(inv[g], axis=0)
            md = jnp.concatenate([jnp.where(lane // W == t, m, 0.0) for t in range(per)], axis=0)
            mh, ml = halves(md)
            x = jnp.concatenate([jnp.where(lane // W == k, unit, hw[per * g + t, r0:r0 + W, :]) for t in range(per)], axis=0)
            xh, xl = halves(x)
            x = dot(jnp.concatenate([mh, mh], axis=1), jnp.concatenate([xh, xl], axis=0)) + dot(ml, xh)
            xh, xl = halves(x)
            for t in range(per):
                n = per * g + t
                lo = slice(W * t, W * t + W)
                hw[n, r0:r0 + W, :] = jnp.where(lane < r0 + W, x[lo], 0.0)
                if k < per - 1:
                    lhs = jnp.concatenate([xh[lo], xh[lo], xl[lo]], axis=0)
                    rhs = jnp.concatenate([xh[lo], xl[lo], xh[lo]], axis=0)
                    upd = dot(lhs, rhs, ((0,), (0,)))[r0 + W:]
                    rest = hw[n, r0 + W:, :]
                    at = lax.broadcasted_iota(jnp.int32, rest.shape, 1) // W
                    hw[n, r0 + W:, :] = jnp.where(at == k, 0.0, rest) - upd
    for n in range(nodes):
        ch, cl = halves(c_ref[base + n])
        wh, wl = halves(hw[n])
        both = dot(jnp.concatenate([ch, ch], 1), jnp.concatenate([wh, wl], 1), ((1,), (1,)))
        out_ref[base + n] = both + dot(cl, wh, ((1,), (1,)))


LEAF = 512
vm = pl.BlockSpec(memory_space=pltpu.VMEM)


def skeleton_points(points_ref, skeleton_ref, gathered):
    for n0 in range(0, NN, 8):
        at = skeleton_ref[n0:n0 + 8, :]
        inside, tile = at % R, at // R
        for c in range(3):
            got = None
            for t in range(LEAF // R):
                part = points_ref[c, n0:n0 + 8, t * R:(t + 1) * R]
                part = jnp.take_along_axis(part, inside, axis=1)
                got = part if got is None else jnp.where(tile == t, part, got)
            gathered[c, n0:n0 + 8, :] = got


def skeleton_columns(gathered, columns, base):
    for c in range(3):
        for n0 in range(0, NN, 8):
            turned = gathered[c, n0:n0 + 8, :].T
            for n in range(8):
                columns[base + n0 + n, c] = jnp.broadcast_to(turned[:, n:n + 1], (R, R))


def one_block(columns, rows_ref, split_ref, node, far):
    near_x, near_y, near_g = columns[node, 0], columns[node, 1], columns[node, 2]
    parts = []
    for t in range(LEAF // R):
        lanes = slice(t * R, (t + 1) * R)
        dx = near_x - rows_ref[far, 0:1, lanes]
        dy = near_y - rows_ref[far, 1:2, lanes]
        parts.append(lax.rsqrt(dx * dx + dy * dy + near_g * rows_ref[far, 2:3, lanes]))
    kh, kl = halves(jnp.concatenate(parts, axis=1))
    high = dot(kh, split_ref[far])
    return high[:, :R] + (high[:, R:] + dot(kl, split_ref[far, :, 0:R]))


def chosen_block(columns, rows_ref, split_ref, node, far, allowed):
    inside = (far >= 0) & (far < NN) & allowed
    block = one_block(columns, rows_ref, split_ref, node, jnp.where(inside, far, 0))
    return jnp.where(inside, block, 0.0)


MESH = pl.DeviceIdType.MESH
NX, NZ, PACK, CUT = 4, 8, 72, 56
SCALE = LEAF ** (-0.5)


def to_row(source, target, send, recv, row):
    return pltpu.make_async_remote_copy(
        src_ref=source, dst_ref=target, send_sem=send, recv_sem=recv,
        device_id=(lax.axis_index("level"), row), device_id_type=MESH,
    )


def climb_kernel(owner_ref, points_hbm, skeleton_hbm, near_hbm, coupling_hbm, panels_hbm, transfer_hbm,
                 solved,
                 points, rows, skeleton, near, panels, split, transfer, lower, wide, rise, coupling, by_z, by_x,
                 gathered, far_gathered, far_near_vmem, far_near, columns, lent, lent_in, mate, below, base, carried, hw,
                 fetch_sem, near_sem, ask_send, ask_receive, halo_send, halo_receive, up_send, up_receive,
                 pair_send, pair_receive, lower_send, lower_receive,
                 x_send, x_receive, z_send, z_receive, xx_send, xx_receive, zz_send, zz_receive):
    level, me = lax.axis_index("level"), lax.axis_index("row")
    top, count = lax.axis_size("level") - 1, NX * NZ
    z, x = me // NX, me % NX
    previous, following = (me + count - 1) % count, (me + 1) % count
    along_x = [z * NX + (x + d) % NX for d in range(1, NX)]
    along_z = [(z + d) % NZ * NX + x for d in range(1, NZ)]

    fetches = [
        pltpu.make_async_copy(source, target, fetch_sem.at[i])
        for i, (source, target) in enumerate(
            ((points_hbm, points), (skeleton_hbm, skeleton), (near_hbm, near), (coupling_hbm, coupling), (panels_hbm, panels), (transfer_hbm, transfer))
        )
    ]
    for copy in fetches:
        copy.start()

    barrier = pltpu.get_barrier_semaphore()
    peers = [(level, r) for r in [previous, following] + along_z + along_x]
    peers += [((level + step) % (top + 1), me) for step in (1, 2, top - 1, top)]
    odd = level % 2 == 1
    for device in peers:
        pl.semaphore_signal(barrier, inc=1, device_id=device, device_id_type=MESH)

    for i in (0, 1, 3):
        fetches[i].wait()
    skeleton_points(points, skeleton, gathered)
    body, diagonal = packed_coupling(coupling[...])
    by_z[x, z] = body[0:CUT, :]
    by_x[z, x, 0:64 - CUT, :] = body[CUT:64, :]
    by_x[z, x, 64 - CUT:PACK - CUT, :] = diagonal
    pl.semaphore_wait(barrier, len(peers))

    asks = []
    for i, (source, target) in enumerate(((gathered, far_gathered), (near_hbm, far_near_vmem))):
        asks.append(to_row(source, target.at[0], ask_send.at[0, i], ask_receive.at[0, i], following))
        asks.append(to_row(source, target.at[1], ask_send.at[1, i], ask_receive.at[1, i], previous))
    first = [to_row(by_z.at[x, z], by_z.at[x, z], z_send.at[i], z_receive.at[i], r) for i, r in enumerate(along_z)]
    first += [to_row(by_x.at[z, x], by_x.at[z, x], x_send.at[i], x_receive.at[i], r) for i, r in enumerate(along_x)]
    second = [to_row(by_z.at[x], by_z.at[x], xx_send.at[i], xx_receive.at[i], r) for i, r in enumerate(along_x)]
    second += [to_row(by_x.at[z], by_x.at[z], zz_send.at[i], zz_receive.at[i], r) for i, r in enumerate(along_z)]
    for copy in asks + first:
        copy.start()

    def to_level(source, target, send, recv, step):
        return pltpu.make_async_remote_copy(
            src_ref=source, dst_ref=target, send_sem=send, recv_sem=recv,
            device_id=(level + step, me), device_id_type=MESH,
        )

    hand_down = to_level(transfer_hbm, lower, lower_send, lower_receive, 1)

    @pl.when(jnp.logical_not(odd))
    def _():
        hand_down.start()

    for n in range(NN):
        for c in range(3):
            rows[n, c:c + 1, :] = points[c, n:n + 1, :]
    skeleton_columns(gathered, columns, 2 * NN)
    fetches[2].wait()
    fetches[4].wait()

    def divide(n, carry):
        high, low = halves(panels[n])
        split[n] = jnp.concatenate([high, low], axis=1)
        return carry

    lax.fori_loop(0, NN, divide, 0)

    for copy in asks:
        copy.wait()
    turn = pltpu.make_async_copy(far_near_vmem, far_near, near_sem)
    turn.start()
    skeleton_columns(far_gathered.at[0], columns, 0)
    skeleton_columns(far_gathered.at[1], columns, NN)
    turn.wait()

    def halo(n, side):
        return to_row(lent.at[side, n], lent_in.at[side, n], halo_send.at[side, n], halo_receive.at[side, n],
                      following if side else previous)

    def lend(n, carry):
        for side, offset, allowed in ((0, 2 * NN, me > 0), (1, 0, me < count - 1)):
            total = None
            for slot in range(2):
                block = chosen_block(columns, rows, split, side * NN + n, far_near[side, slot, n] - offset, allowed)
                total = block if total is None else total + block
            lent[side, n] = total * SCALE
        halo(n, 0).start()
        halo(n, 1).start()
        return carry

    lax.fori_loop(0, NN, lend, 0)
    for copy in first:
        copy.wait()
    for copy in second:
        copy.start()

    fetches[5].wait()

    def widen(n, carry):
        high, low = halves(transfer[n])
        wide[n] = jnp.concatenate([high, high, low], axis=1)
        rise[n] = wide[n]
        return carry

    lax.fori_loop(0, NN, widen, 0)

    @pl.when(odd)
    def _():
        hand_down.wait_recv()

        def both_levels(n, carry):
            high, low = halves(lower[n])
            high, low = halves(dot(wide[n], jnp.concatenate([high, low, high], axis=0)))
            rise[n] = jnp.concatenate([high, high, low], axis=1)
            return carry

        lax.fori_loop(0, NN, both_levels, 0)

    def pair(n):
        return to_level(base.at[n], mate.at[n], pair_send.at[n], pair_receive.at[n], 1)

    def up(n):
        return to_level(carried.at[n], below.at[n], up_send.at[0, n], up_receive.at[n], 2)

    def across(n):
        return to_level(below.at[n], below.at[n], up_send.at[1, n], up_receive.at[n], -1)

    def times(matrix, block):
        high, low = halves(block)
        return dot(matrix, jnp.concatenate([high, low, high], axis=0))

    def climb(n, carry):
        mine = one_block(columns, rows, split, 2 * NN + n, n)
        for slot in range(2):
            mine = mine + chosen_block(columns, rows, split, 2 * NN + n, near[slot, n] - NN, True)
        mine = mine * SCALE
        halo(n, 0).wait_recv()
        halo(n, 1).wait_recv()
        local = mine + lent_in[0, n] + lent_in[1, n]
        base[n] = local
        carried[n] = local

        @pl.when(jnp.logical_not(odd))
        def _():
            pair(n).start()

        @pl.when(odd)
        def _():
            pair(n).wait_recv()
            carried[n] = carried[n] + times(wide[n], mate[n])

            @pl.when(level >= 2)
            def _():
                up(n).wait_recv()
                across(n).start()
                carried[n] = carried[n] + times(rise[n], below[n])

            @pl.when(level < top)
            def _():
                up(n).start()

        return carry

    def follow(n, carry):
        up(n).wait_recv()
        carried[n] = carried[n] + times(rise[n], below[n])
        return carry

    lax.fori_loop(0, NN, climb, 0)

    @pl.when(jnp.logical_not(odd) & (level >= 2))
    def _():
        lax.fori_loop(0, NN, follow, 0)

    for copy in second:
        copy.wait()
    eliminate(8, 0, NN, owner_ref, carried, by_z, by_x, solved, hw)

    def settle(n, carry):
        halo(n, 0).wait_send()
        halo(n, 1).wait_send()

        @pl.when(jnp.logical_not(odd))
        def _():
            pair(n).wait_send()

        @pl.when(odd & (level < top))
        def _():
            up(n).wait_send()

        @pl.when(odd & (level >= 2))
        def _():
            across(n).wait_send()

        return carry

    lax.fori_loop(0, NN, settle, 0)

    @pl.when(jnp.logical_not(odd))
    def _():
        hand_down.wait_send()


def climb_levels(owner, points, skeleton, near, coupling, panels, transfer):
    hbm = pl.BlockSpec(memory_space=pltpu.HBM)
    shape = jax.ShapeDtypeStruct
    dma = pltpu.SemaphoreType.DMA
    v = pltpu.VMEM
    return pl.pallas_call(
        climb_kernel,
        out_shape=shape((NN, R, R), F32),
        in_specs=[pl.BlockSpec(memory_space=pltpu.SMEM)] + [hbm] * 6,
        out_specs=vm,
        scratch_shapes=[
            v(points.shape, F32), v((NN, 3, LEAF), F32), v(skeleton.shape, jnp.int32), pltpu.SMEM(near.shape, jnp.int32), v(panels.shape, F32),
            v((NN, LEAF, 2 * R), BF16), v((NN, R, R), F32), v((NN, R, R), F32), v((NN, R, 3 * R), BF16), v((NN, R, 3 * R), BF16), v((R, R), F32),
            v((NX, NZ, CUT, R), F32), v((NZ, NX, PACK - CUT, R), F32),
            v((3, NN, R), F32), v((2, 3, NN, R), F32), v((2,) + near.shape, jnp.int32),
            pltpu.SMEM((2,) + near.shape, jnp.int32), v((3 * NN, 3, R, R), F32),
            v((2, NN, R, R), F32), v((2, NN, R, R), F32), v((NN, R, R), F32), v((NN, R, R), F32),
            v((NN, R, R), F32), v((NN, R, R), F32), v((NN, R, R), F32),
            dma((6,)), dma, dma((2, 2)), dma((2, 2)), dma((2, NN)), dma((2, NN)), dma((2, NN)), dma((NN,)), dma((NN,)), dma((NN,)), dma, dma,
            dma((NX - 1,)), dma((NX - 1,)), dma((NZ - 1,)), dma((NZ - 1,)),
            dma((NX - 1,)), dma((NX - 1,)), dma((NZ - 1,)), dma((NZ - 1,)),
        ],
        compiler_params=pltpu.CompilerParams(collective_id=0, has_side_effects=True, vmem_limit_bytes=58 << 20),
        name="climb",
    )(owner, points, skeleton, near, coupling, panels, transfer)


def per_device(points, panels, near_nodes, skeleton, owner_map, transfer, coupling):
    return climb_levels(
        owner_map[0, :, 0], points[0].transpose(1, 0, 2), skeleton[0], near_nodes[0].T, coupling[0], panels[0], transfer[0]
    )[None]


def solution(mesh):
    return jax.shard_map(
        per_device,
        mesh=mesh,
        in_specs=(
            P("level", "row", None, None),
            P("level", "row", None, None),
            P("level", "row", None),
            P("level", "row", None),
            P("level", "row", None),
            P("level", "row", None, None),
            P("level", "row", None),
        ),
        out_specs=P("level", "row", None, None),
        check_vma=False,
    )
```

```python
import jax
import jax.numpy as jnp
from jax import lax
from jax.experimental import pallas as pl
from jax.experimental.pallas import tpu as pltpu
from jax.sharding import PartitionSpec as P
F32, BF16 = jnp.float32, jnp.bfloat16
NN, R, W = 16, 128, 32

def halves(x):
    high = x.astype(BF16)
    return high, (x - high.astype(F32)).astype(BF16)

def dot(a, b, dims=((1,), (0,))):
    return lax.dot_general(a, b, (dims, ((), ())), preferred_element_type=F32)

def spread_row(x, row):
    return jnp.broadcast_to(x[row:row + 1, :], x.shape)

def lane_pick(x, index):
    return jnp.take_along_axis(x, index, axis=1)

def invert_factors(diag, step):
    groups, parts = len(diag), W // 8
    lane = lax.broadcasted_iota(jnp.int32, (8, R), 1)
    row = lax.broadcasted_iota(jnp.int32, (8, R), 0)
    seg = (lane // W) * W
    within = lane % W
    rest = [list(d) for d in diag]
    work = [[jnp.where(within == row + 8 * q, 1.0, 0.0).astype(F32) for q in range(parts)] for _ in range(groups)]
    for j in range(0, W, step):
        q0 = j // 8
        for g in range(groups):
            cols = [{q: lane_pick(rest[g][q], seg + (j + t)) for q in range(q0, parts)} for t in range(step)]
            rows = [spread_row(rest[g][q0], (j + t) % 8) for t in range(step)]
            wrows = [spread_row(work[g][q0], (j + t) % 8) for t in range(step)]
            for t in range(step):
                at = (j + t) % 8
                scale = lax.rsqrt(spread_row(cols[t][q0], at))
                left = {q: cols[t][q] * scale for q in range(q0, parts)}
                right = rows[t] * scale
                wright = wrows[t] * scale
                for u in range(t + 1, step):
                    f = spread_row(left[q0], (j + u) % 8)
                    rows[u] = rows[u] - f * right
                    wrows[u] = wrows[u] - f * wright
                    for q in range(q0, parts):
                        cols[u][q] = cols[u][q] - left[q] * f
                for q in range(q0, parts):
                    l = jnp.where(row > at, left[q], 0.0) if q == q0 else left[q]
                    rest[g][q] = rest[g][q] - l * right
                    work[g][q] = work[g][q] - l * wright
                work[g][q0] = jnp.where(row == at, wright, work[g][q0])
    return work

def packed_coupling(s):
    row = lax.broadcasted_iota(jnp.int32, (64, R), 0)
    lane = lax.broadcasted_iota(jnp.int32, (64, R), 1)
    low, high = s[64:R, :], s[0:64, :]
    turned = pltpu.roll(high, 64, 1)
    body = jnp.where(lane - 64 > row, turned, jnp.where(lane - 64 == row, 0.5 * low, low))
    diagonal = jnp.sum(jnp.where(lane == row, 0.5 * high, 0.0), axis=0, keepdims=True)
    return body, jnp.broadcast_to(diagonal, (8, R))


def half_coupling(packed):
    row = lax.broadcasted_iota(jnp.int32, (64, R), 0)
    lane = lax.broadcasted_iota(jnp.int32, (64, R), 1)
    body = packed[0:64, :]
    turned = pltpu.roll(body, 64, 1)
    diagonal = jnp.broadcast_to(packed[64:65, :], (64, R))
    top = jnp.where(lane < 64, jnp.where(lane > row, turned, jnp.where(lane == row, diagonal, 0.0)), 0.0)
    low = jnp.where(lane - 64 <= row, body, 0.0)
    return jnp.concatenate([top, low], axis=0)


def eliminate(step, base, nodes, owner_ref, c_ref, by_z, by_x, out_ref, hw):
    for n in range(nodes):
        owner = owner_ref[base + n]
        half = half_coupling(jnp.concatenate([by_z[owner % 4, owner // 4], by_x[owner // 4, owner % 4]], axis=0))
        hw[n] = half + half.T + hw[n]
    lane = lax.broadcasted_iota(jnp.int32, (W, R), 1)
    row = lax.broadcasted_iota(jnp.int32, (W, R), 0)
    per = R // W
    groups = nodes // per
    for k in range(per):
        r0 = W * k
        diag = []
        for g in range(groups):
            packed = None
            for t in range(per):
                x = hw[per * g + t, r0:r0 + W, :]
                if t != k:
                    x = pltpu.roll(x, (W * (t - k)) % R, 1)
                packed = x if packed is None else jnp.where(lane // W == t, x, packed)
            diag.append([packed[8 * q:8 * q + 8] for q in range(W // 8)])
        inv = invert_factors(diag, step)
        unit = jnp.where(lane - r0 == row, 1.0, 0.0).astype(F32)
        for g in range(groups):
            m = jnp.concatenate(inv[g], axis=0)
            md = jnp.concatenate([jnp.where(lane // W == t, m, 0.0) for t in range(per)], axis=0)
            mh, ml = halves(md)
            x = jnp.concatenate([jnp.where(lane // W == k, unit, hw[per * g + t, r0:r0 + W, :]) for t in range(per)], axis=0)
            xh, xl = halves(x)
            x = dot(jnp.concatenate([mh, mh], axis=1), jnp.concatenate([xh, xl], axis=0)) + dot(ml, xh)
            xh, xl = halves(x)
            for t in range(per):
                n = per * g + t
                lo = slice(W * t, W * t + W)
                hw[n, r0:r0 + W, :] = jnp.where(lane < r0 + W, x[lo], 0.0)
                if k < per - 1:
                    lhs = jnp.concatenate([xh[lo], xh[lo], xl[lo]], axis=0)
                    rhs = jnp.concatenate([xh[lo], xl[lo], xh[lo]], axis=0)
                    upd = dot(lhs, rhs, ((0,), (0,)))[r0 + W:]
                    rest = hw[n, r0 + W:, :]
                    at = lax.broadcasted_iota(jnp.int32, rest.shape, 1) // W
                    hw[n, r0 + W:, :] = jnp.where(at == k, 0.0, rest) - upd
    for n in range(nodes):
        ch, cl = halves(c_ref[base + n])
        wh, wl = halves(hw[n])
        both = dot(jnp.concatenate([ch, ch], 1), jnp.concatenate([wh, wl], 1), ((1,), (1,)))
        out_ref[base + n] = both + dot(cl, wh, ((1,), (1,)))


LEAF = 512
vm = pl.BlockSpec(memory_space=pltpu.VMEM)


def skeleton_points(points_ref, skeleton_ref, gathered):
    for n0 in range(0, NN, 8):
        at = skeleton_ref[n0:n0 + 8, :]
        inside, tile = at % R, at // R
        for c in range(3):
            got = None
            for t in range(LEAF // R):
                part = points_ref[c, n0:n0 + 8, t * R:(t + 1) * R]
                part = jnp.take_along_axis(part, inside, axis=1)
                got = part if got is None else jnp.where(tile == t, part, got)
            gathered[c, n0:n0 + 8, :] = got


def skeleton_columns(gathered, columns, base):
    for c in range(3):
        for n0 in range(0, NN, 8):
            turned = gathered[c, n0:n0 + 8, :].T
            for n in range(8):
                columns[base + n0 + n, c] = jnp.broadcast_to(turned[:, n:n + 1], (R, R))


def one_block(columns, rows_ref, split_ref, node, far):
    near_x, near_y, near_g = columns[node, 0], columns[node, 1], columns[node, 2]
    parts = []
    for t in range(LEAF // R):
        lanes = slice(t * R, (t + 1) * R)
        dx = near_x - rows_ref[far, 0:1, lanes]
        dy = near_y - rows_ref[far, 1:2, lanes]
        parts.append(lax.rsqrt(dx * dx + dy * dy + near_g * rows_ref[far, 2:3, lanes]))
    kh, kl = halves(jnp.concatenate(parts, axis=1))
    high = dot(kh, split_ref[far])
    return high[:, :R] + (high[:, R:] + dot(kl, split_ref[far, :, 0:R]))


def chosen_block(columns, rows_ref, split_ref, node, far, allowed):
    inside = (far >= 0) & (far < NN) & allowed
    block = one_block(columns, rows_ref, split_ref, node, jnp.where(inside, far, 0))
    return jnp.where(inside, block, 0.0)


MESH = pl.DeviceIdType.MESH
NX, NZ, PACK, CUT = 4, 8, 72, 56
SCALE = LEAF ** (-0.5)


def to_row(source, target, send, recv, row):
    return pltpu.make_async_remote_copy(
        src_ref=source, dst_ref=target, send_sem=send, recv_sem=recv,
        device_id=(lax.axis_index("level"), row), device_id_type=MESH,
    )


def climb_kernel(owner_ref, points_hbm, skeleton_hbm, near_hbm, coupling_hbm, panels_hbm, transfer_hbm,
                 solved,
                 points, rows, skeleton, near, panels, split, transfer, lower, wide, rise, coupling, by_z, by_x,
                 gathered, far_gathered, far_near_vmem, far_near, columns, lent, lent_in, mate, below, base, carried, hw,
                 fetch_sem, near_sem, ask_send, ask_receive, halo_send, halo_receive, up_send, up_receive,
                 pair_send, pair_receive, lower_send, lower_receive,
                 x_send, x_receive, z_send, z_receive, xx_send, xx_receive, zz_send, zz_receive):
    level, me = lax.axis_index("level"), lax.axis_index("row")
    top, count = lax.axis_size("level") - 1, NX * NZ
    z, x = me // NX, me % NX
    previous, following = (me + count - 1) % count, (me + 1) % count
    along_x = [z * NX + (x + d) % NX for d in range(1, NX)]
    along_z = [(z + d) % NZ * NX + x for d in range(1, NZ)]

    fetches = [
        pltpu.make_async_copy(source, target, fetch_sem.at[i])
        for i, (source, target) in enumerate(
            ((points_hbm, points), (skeleton_hbm, skeleton), (near_hbm, near), (coupling_hbm, coupling), (panels_hbm, panels), (transfer_hbm, transfer))
        )
    ]
    for copy in fetches:
        copy.start()

    barrier = pltpu.get_barrier_semaphore()
    peers = [(level, r) for r in [previous, following] + along_z + along_x]
    peers += [((level + step) % (top + 1), me) for step in (1, 2, top - 1, top)]
    odd = level % 2 == 1
    for device in peers:
        pl.semaphore_signal(barrier, inc=1, device_id=device, device_id_type=MESH)

    for i in (0, 1, 3):
        fetches[i].wait()
    skeleton_points(points, skeleton, gathered)
    body, diagonal = packed_coupling(coupling[...])
    by_z[x, z] = body[0:CUT, :]
    by_x[z, x, 0:64 - CUT, :] = body[CUT:64, :]
    by_x[z, x, 64 - CUT:PACK - CUT, :] = diagonal
    pl.semaphore_wait(barrier, len(peers))

    asks = []
    for i, (source, target) in enumerate(((gathered, far_gathered), (near_hbm, far_near_vmem))):
        asks.append(to_row(source, target.at[0], ask_send.at[0, i], ask_receive.at[0, i], following))
        asks.append(to_row(source, target.at[1], ask_send.at[1, i], ask_receive.at[1, i], previous))
    first = [to_row(by_z.at[x, z], by_z.at[x, z], z_send.at[i], z_receive.at[i], r) for i, r in enumerate(along_z)]
    first += [to_row(by_x.at[z, x], by_x.at[z, x], x_send.at[i], x_receive.at[i], r) for i, r in enumerate(along_x)]
    second = [to_row(by_z.at[x], by_z.at[x], xx_send.at[i], xx_receive.at[i], r) for i, r in enumerate(along_x)]
    second += [to_row(by_x.at[z], by_x.at[z], zz_send.at[i], zz_receive.at[i], r) for i, r in enumerate(along_z)]
    for copy in asks + first:
        copy.start()

    def to_level(source, target, send, recv, step):
        return pltpu.make_async_remote_copy(
            src_ref=source, dst_ref=target, send_sem=send, recv_sem=recv,
            device_id=(level + step, me), device_id_type=MESH,
        )

    hand_down = to_level(transfer_hbm, lower, lower_send, lower_receive, 1)

    @pl.when(jnp.logical_not(odd))
    def _():
        hand_down.start()

    for n in range(NN):
        for c in range(3):
            rows[n, c:c + 1, :] = points[c, n:n + 1, :]
    skeleton_columns(gathered, columns, 2 * NN)
    fetches[2].wait()
    fetches[4].wait()

    def divide(n, carry):
        high, low = halves(panels[n])
        split[n] = jnp.concatenate([high, low], axis=1)
        return carry

    lax.fori_loop(0, NN, divide, 0)

    for copy in asks:
        copy.wait()
    turn = pltpu.make_async_copy(far_near_vmem, far_near, near_sem)
    turn.start()
    skeleton_columns(far_gathered.at[0], columns, 0)
    skeleton_columns(far_gathered.at[1], columns, NN)
    turn.wait()

    def halo(n, side):
        return to_row(lent.at[side, n], lent_in.at[side, n], halo_send.at[side, n], halo_receive.at[side, n],
                      following if side else previous)

    def lend(n, carry):
        for side, offset, allowed in ((0, 2 * NN, me > 0), (1, 0, me < count - 1)):
            total = None
            for slot in range(2):
                block = chosen_block(columns, rows, split, side * NN + n, far_near[side, slot, n] - offset, allowed)
                total = block if total is None else total + block
            lent[side, n] = total * SCALE
            halo(n, side).start()
        return carry

    lax.fori_loop(0, NN, lend, 0)
    for copy in first:
        copy.wait()
    for copy in second:
        copy.start()

    fetches[5].wait()

    def widen(n, carry):
        high, low = halves(transfer[n])
        wide[n] = jnp.concatenate([high, high, low], axis=1)
        rise[n] = wide[n]
        return carry

    lax.fori_loop(0, NN, widen, 0)

    @pl.when(odd)
    def _():
        hand_down.wait_recv()

        def both_levels(n, carry):
            high, low = halves(lower[n])
            high, low = halves(dot(wide[n], jnp.concatenate([high, low, high], axis=0)))
            rise[n] = jnp.concatenate([high, high, low], axis=1)
            return carry

        lax.fori_loop(0, NN, both_levels, 0)

    def pair(n):
        return to_level(base.at[n], mate.at[n], pair_send.at[n], pair_receive.at[n], 1)

    def up(n):
        return to_level(carried.at[n], below.at[n], up_send.at[0, n], up_receive.at[n], 2)

    def across(n):
        return to_level(below.at[n], below.at[n], up_send.at[1, n], up_receive.at[n], -1)

    def times(matrix, block):
        high, low = halves(block)
        return dot(matrix, jnp.concatenate([high, low, high], axis=0))

    def weigh(n):
        ch, cl = halves(carried[n])
        gram = dot(jnp.concatenate([ch, ch, cl], 0), jnp.concatenate([ch, cl, ch], 0), ((0,), (0,)))
        hw[n] = gram * (1.0 / R)

    def climb(n, carry):
        mine = one_block(columns, rows, split, 2 * NN + n, n)
        for slot in range(2):
            mine = mine + chosen_block(columns, rows, split, 2 * NN + n, near[slot, n] - NN, True)
        mine = mine * SCALE
        halo(n, 0).wait_recv()
        halo(n, 1).wait_recv()
        local = mine + lent_in[0, n] + lent_in[1, n]
        base[n] = local
        carried[n] = local

        @pl.when(jnp.logical_not(odd))
        def _():
            pair(n).start()

        @pl.when(odd)
        def _():
            pair(n).wait_recv()
            carried[n] = carried[n] + times(wide[n], mate[n])

            @pl.when(level >= 2)
            def _():
                up(n).wait_recv()
                across(n).start()
                carried[n] = carried[n] + times(rise[n], below[n])

            @pl.when(level < top)
            def _():
                up(n).start()

            weigh(n)

        @pl.when(level == 0)
        def _():
            weigh(n)

        return carry

    def follow(n, carry):
        up(n).wait_recv()
        carried[n] = carried[n] + times(rise[n], below[n])
        weigh(n)
        return carry

    lax.fori_loop(0, NN, climb, 0)

    @pl.when(jnp.logical_not(odd) & (level >= 2))
    def _():
        lax.fori_loop(0, NN, follow, 0)

    for copy in second:
        copy.wait()
    eliminate(8, 0, NN, owner_ref, carried, by_z, by_x, solved, hw)

    def settle(n, carry):
        halo(n, 0).wait_send()
        halo(n, 1).wait_send()

        @pl.when(jnp.logical_not(odd))
        def _():
            pair(n).wait_send()

        @pl.when(odd & (level < top))
        def _():
            up(n).wait_send()

        @pl.when(odd & (level >= 2))
        def _():
            across(n).wait_send()

        return carry

    lax.fori_loop(0, NN, settle, 0)

    @pl.when(jnp.logical_not(odd))
    def _():
        hand_down.wait_send()


def climb_levels(owner, points, skeleton, near, coupling, panels, transfer):
    hbm = pl.BlockSpec(memory_space=pltpu.HBM)
    shape = jax.ShapeDtypeStruct
    dma = pltpu.SemaphoreType.DMA
    v = pltpu.VMEM
    return pl.pallas_call(
        climb_kernel,
        out_shape=shape((NN, R, R), F32),
        in_specs=[pl.BlockSpec(memory_space=pltpu.SMEM)] + [hbm] * 6,
        out_specs=vm,
        scratch_shapes=[
            v(points.shape, F32), v((NN, 3, LEAF), F32), v(skeleton.shape, jnp.int32), pltpu.SMEM(near.shape, jnp.int32), v(panels.shape, F32),
            v((NN, LEAF, 2 * R), BF16), v((NN, R, R), F32), v((NN, R, R), F32), v((NN, R, 3 * R), BF16), v((NN, R, 3 * R), BF16), v((R, R), F32),
            v((NX, NZ, CUT, R), F32), v((NZ, NX, PACK - CUT, R), F32),
            v((3, NN, R), F32), v((2, 3, NN, R), F32), v((2,) + near.shape, jnp.int32),
            pltpu.SMEM((2,) + near.shape, jnp.int32), v((3 * NN, 3, R, R), F32),
            v((2, NN, R, R), F32), v((2, NN, R, R), F32), v((NN, R, R), F32), v((NN, R, R), F32),
            v((NN, R, R), F32), v((NN, R, R), F32), v((NN, R, R), F32),
            dma((6,)), dma, dma((2, 2)), dma((2, 2)), dma((2, NN)), dma((2, NN)), dma((2, NN)), dma((NN,)), dma((NN,)), dma((NN,)), dma, dma,
            dma((NX - 1,)), dma((NX - 1,)), dma((NZ - 1,)), dma((NZ - 1,)),
            dma((NX - 1,)), dma((NX - 1,)), dma((NZ - 1,)), dma((NZ - 1,)),
        ],
        compiler_params=pltpu.CompilerParams(collective_id=0, has_side_effects=True, vmem_limit_bytes=58 << 20),
        name="climb",
    )(owner, points, skeleton, near, coupling, panels, transfer)


def per_device(points, panels, near_nodes, skeleton, owner_map, transfer, coupling):
    return climb_levels(
        owner_map[0, :, 0], points[0].transpose(1, 0, 2), skeleton[0], near_nodes[0].T, coupling[0], panels[0], transfer[0]
    )[None]


def solution(mesh):
    return jax.shard_map(
        per_device,
        mesh=mesh,
        in_specs=(
            P("level", "row", None, None),
            P("level", "row", None, None),
            P("level", "row", None),
            P("level", "row", None),
            P("level", "row", None),
            P("level", "row", None, None),
            P("level", "row", None),
        ),
        out_specs=P("level", "row", None, None),
        check_vma=False,
    )
```
